32 devices in a mesh: dp: 8 (over y, x, core), seq: 4 (over z).
Axes of the slice: x: 2, y: 2, z: 4, core: 2. Of those that a mesh axis runs over, the one named last changes fastest.
Arguments:
- hidden_in: bfloat16 [8, 512, 1024], P('dp', 'seq'), may hold values from -6 to 6
- out_grad: bfloat16 [8, 512, 1024], P('dp', 'seq'), may hold values from -6 to 6
- norm_params: bfloat16 [4096], P(('dp', 'seq')), may hold values from -1 to 1.625
- biases: bfloat16 [8192], P(('dp', 'seq')), may hold values from -1.796875 to 1.796875
- attn_in: bfloat16 [1024, 3072], P('dp', 'seq'), may hold values from -0.1875 to 0.1875
- attn_out: bfloat16 [1024, 1024], P('seq', 'dp'), may hold values from -1 to 1
- mlp_up: bfloat16 [1024, 4096], P('dp', 'seq'), may hold values from -0.1875 to 0.1875
- mlp_down: bfloat16 [4096, 1024], P('seq', 'dp'), may hold values from -0.09375 to 0.09375
Outputs:
- layer_out: bfloat16 [8, 512, 1024], P('dp', 'seq')
- grad_input: bfloat16 [8, 512, 1024], P('dp', 'seq')
- grad_norm: float32 [4096], P(('dp', 'seq'))
- grad_bias: float32 [8192], P(('dp', 'seq'))
- grad_attn_in: float32 [1024, 3072], P('dp', 'seq')
- grad_attn_out: float32 [1024, 1024], P('seq', 'dp')
- grad_up: float32 [1024, 4096], P('dp', 'seq')
- grad_down: float32 [4096, 1024], P('seq', 'dp')
The draws below stay inside these ranges and needn't reach their ends.
All inputs are finite; a program needn't handle non-finite values.
Results may differ from the reference program's by a relative error of at most 0.011.
Values may be sent and summed in bfloat16 or wider, within the bound.
A program may use at most 40 MiB of HBM per device.

```python
import math
import jax
import jax.numpy as jnp
from jax import lax

D = 1024
H = 16
HD = 64
FF = 4096
ROT = 16
LEN = 512
SEQS = 8


def draw_norm_params(key, part):
    key = jax.random.fold_in(key, 7)
    gain_key, shift_key = jax.random.split(key)
    gain_rows = jax.random.uniform(gain_key, (2, 1, D), jnp.float32, 0.5, 1.5)
    shifts = jnp.clip(0.3 * jax.random.normal(shift_key, (2, 1, D), jnp.float32), -0.9, 0.9)
    return jnp.concatenate([gain_rows, shifts], axis=1).reshape(4 * D).astype(jnp.bfloat16)


def shard_levels(stream_key, dims, cuts, least, high):
    level, own = 1.0, jax.random.fold_in(stream_key, 6)
    for axis_at, parts in cuts:
        heights = jnp.exp(jax.random.uniform(jax.random.fold_in(own, axis_at), (parts,), jnp.float32, least / len(cuts), high / len(cuts)))
        level = level * jnp.repeat(heights, dims[axis_at] // parts).reshape([-1 if axis == axis_at else 1 for axis in range(len(dims))])
    return level


def scatter_about(rng, dims, scale, most, cuts=(), kind=jnp.bfloat16):
    drawn = jax.random.normal(rng, dims, jnp.float32) * scale
    if len(cuts) > 0:
        drawn = shard_levels(rng, dims, cuts, -0.22, 0.18) * drawn
    return jnp.clip(drawn, min=-most, max=most).astype(kind)


def setup_inputs(seed: int = 0) -> dict:
    seeds = jax.random.split(jax.random.key(seed), 9)
    hidden_in = scatter_about(seeds[0], (SEQS, LEN, D), 1.0, 6.0, ((0, 8), (1, 4)))
    out_grad = scatter_about(seeds[1], (SEQS, LEN, D), 1.0, 6.0, ((0, 8), (1, 4)))
    norm_params = draw_norm_params(jax.random.fold_in(seeds[8], 71), 0)
    biases = scatter_about(seeds[3], (4 * D + FF,), 0.3, 1.796875, ((0, 32),))
    attn_in = scatter_about(seeds[4], (D, 3 * D), D ** -0.5, 0.1875, ((0, 8), (1, 4)))
    attn_out = scatter_about(seeds[5], (D, D), (D // 32) ** -0.5, 1.0, ((0, 4), (1, 8)))
    mlp_up = scatter_about(seeds[6], (D, FF), D ** -0.5, 0.1875, ((0, 8), (1, 4)))
    mlp_down = scatter_about(seeds[7], (FF, D), FF ** -0.5, 0.09375, ((0, 4), (1, 8)))
    return {"hidden_in": hidden_in, "out_grad": out_grad, "norm_params": norm_params, "biases": biases, "attn_in": attn_in, "attn_out": attn_out, "mlp_up": mlp_up, "mlp_down": mlp_down}


@jax.custom_vjp
def low(v):
    return lax.optimization_barrier(v.astype(jnp.bfloat16)).astype(jnp.float32)

@jax.custom_vjp
def low_back(v):
    return v

def low_keep(v):
    return (low(v), None)

def low_pass(kept, grad):
    return (grad,)

def back_keep(v):
    return (v, None)

def back_low(kept, grad):
    return (low(grad),)
low.defvjp(low_keep, low_pass)
low_back.defvjp(back_keep, back_low)
highest = lax.Precision.HIGHEST
norm_eps = 1e-05
masked_score = -1e+30

def rotary_tables(positions):
    half_rot = ROT // 2
    frequency = jnp.power(jnp.float32(10000.0), -2.0 * jnp.arange(half_rot, dtype=jnp.float32) / ROT)
    angles = positions[:, None] * frequency[None, :]
    return (jnp.cos(angles)[:, None, :], jnp.sin(angles)[:, None, :])

def rotate(tensor, cosine_table, sine_table):
    half_rot = ROT // 2
    first_half = tensor[..., :half_rot]
    second = tensor[..., half_rot:ROT]
    untouched = tensor[..., ROT:]
    return jnp.concatenate([first_half * cosine_table - second * sine_table, second * cosine_table + first_half * sine_table, untouched], axis=-1)

def gelu(values):
    return 0.5 * values * (1.0 + jax.scipy.special.erf(values * (1.0 / math.sqrt(2.0))))

def block_forward(inputs, attn_in, attn_out, mlp_up, mlp_down, norm_params, biases, cosine_table, sine_table):
    batch_count = inputs.shape[0]
    average = lax.optimization_barrier(jnp.mean(inputs, axis=-1, keepdims=True))
    centered = inputs - average
    variance = lax.optimization_barrier(jnp.mean(centered * centered, axis=-1, keepdims=True))
    normed = centered * lax.rsqrt(variance + norm_eps)
    attn_rows = low(normed * norm_params[0] + norm_params[1])
    mlp_rows = low(normed * norm_params[2] + norm_params[3])
    triple = low_back(jnp.einsum('gld,de->gle', attn_rows, attn_in, precision=highest) + biases[:3 * D])
    split = triple.reshape(batch_count, LEN, H, 3, HD)
    queries = low(rotate(split[:, :, :, 0], cosine_table, sine_table))
    key_rows = low(rotate(split[:, :, :, 1], cosine_table, sine_table))
    value_rows = low(split[:, :, :, 2])
    scores = low_back(jnp.einsum('gqhe,gkhe->ghqk', queries, key_rows, precision=highest) * HD ** (-0.5))
    causal = jnp.arange(LEN)[:, None] >= jnp.arange(LEN)[None, :]
    scores = jnp.where(causal, scores, masked_score)
    row_max = lax.optimization_barrier(jnp.max(scores, axis=-1, keepdims=True))
    log_total = row_max + jnp.log(lax.optimization_barrier(jnp.sum(jnp.exp(scores - row_max), axis=-1, keepdims=True)))
    attn_probs = low(jnp.exp(scores - log_total))
    mixed_rows = jnp.einsum('ghqk,gkhe->gqhe', attn_probs, value_rows, precision=highest).reshape(batch_count, LEN, D)
    mixed_rows = low(low_back(mixed_rows))
    attended = jnp.einsum('gld,de->gle', mixed_rows, attn_out, precision=highest)
    hidden = low_back(jnp.einsum('gld,df->glf', mlp_rows, mlp_up, precision=highest) + biases[3 * D:3 * D + FF])
    activated = low(gelu(hidden))
    mlp_result = jnp.einsum('glf,fd->gld', activated, mlp_down, precision=highest)
    return inputs + attended + mlp_result + biases[3 * D + FF:]

def reference(hidden_in, out_grad, norm_params, biases, attn_in, attn_out, mlp_up, mlp_down):
    params = (attn_in.astype(jnp.float32), attn_out.astype(jnp.float32), mlp_up.astype(jnp.float32), mlp_down.astype(jnp.float32), norm_params.astype(jnp.float32).reshape(4, D), biases.astype(jnp.float32))
    group_size = 1
    for candidate in range(1, SEQS + 1):
        if SEQS % candidate == 0 and candidate * LEN <= 4096:
            group_size = candidate
    cosine_table, sine_table = rotary_tables(jnp.arange(LEN, dtype=jnp.float32))
    checked = jax.checkpoint(block_forward)

    def whole_forward(inputs, weight_set):
        blocks = inputs.reshape(SEQS // group_size, group_size, LEN, D)

        def advance(carried, seq_block):
            return (carried, checked(seq_block, *weight_set, cosine_table, sine_table))
        unused, results = lax.scan(advance, jnp.zeros((), jnp.float32), blocks)
        return results.reshape(SEQS, LEN, D)
    result, pullback = jax.vjp(whole_forward, hidden_in.astype(jnp.float32), params)
    grad_inputs, weight_grads = pullback(out_grad.astype(jnp.float32))
    return (result.astype(jnp.bfloat16), grad_inputs.astype(jnp.bfloat16), weight_grads[4].reshape(-1), weight_grads[5], weight_grads[0], weight_grads[1], weight_grads[2], weight_grads[3])
```

```python
import functools
import math

import jax
import jax.numpy as jnp
from jax import lax
from jax.experimental import pallas as pl
from jax.experimental.pallas import tpu as pltpu
from jax.sharding import PartitionSpec as P

D = 1024
H = 16
HD = 64
FF = 4096
ROT = 16


norm_eps = 1e-05
masked_score = -1e30


def rotary_tables(positions):
    half_rot = ROT // 2
    frequency = jnp.power(
        jnp.float32(10000.0), -2.0 * jnp.arange(half_rot, dtype=jnp.float32) / ROT
    )
    angles = positions[:, None] * frequency[None, :]
    return (jnp.cos(angles)[:, None, :], jnp.sin(angles)[:, None, :])


def rotate(tensor, cosine_table, sine_table):
    half_rot = ROT // 2
    first_half = tensor[..., :half_rot]
    second = tensor[..., half_rot:ROT]
    untouched = tensor[..., ROT:]
    return jnp.concatenate(
        [
            first_half * cosine_table - second * sine_table,
            second * cosine_table + first_half * sine_table,
            untouched,
        ],
        axis=-1,
    )


def rotate_back(tensor, cosine_table, sine_table):
    half_rot = ROT // 2
    first_half = tensor[..., :half_rot]
    second = tensor[..., half_rot:ROT]
    untouched = tensor[..., ROT:]
    return jnp.concatenate(
        [
            first_half * cosine_table + second * sine_table,
            second * cosine_table - first_half * sine_table,
            untouched,
        ],
        axis=-1,
    )


def gelu(values):
    return 0.5 * values * (1.0 + jax.scipy.special.erf(values * (1.0 / math.sqrt(2.0))))


def gelu_slope(values):
    return 0.5 * (1.0 + jax.scipy.special.erf(values * (1.0 / math.sqrt(2.0)))) + values * jnp.exp(
        -0.5 * values * values
    ) * (1.0 / math.sqrt(2.0 * math.pi))


def score_block(queries, keys_full, causal):
    raw_scores = jnp.einsum(
        "sqhe,skhe->shqk", queries, keys_full, preferred_element_type=jnp.float32
    ) * HD ** (-0.5)
    return jnp.where(causal, raw_scores, masked_score)


def attend_forward(queries, keys_full, values_full, causal):
    scores = score_block(queries, keys_full, causal)
    row_max = jnp.max(scores, axis=-1, keepdims=True)
    log_total = row_max + jnp.log(jnp.sum(jnp.exp(scores - row_max), axis=-1, keepdims=True))
    probs_low = jnp.exp(scores - log_total).astype(jnp.bfloat16)
    mixed_heads = jnp.einsum(
        "shqk,skhe->sqhe", probs_low, values_full, preferred_element_type=jnp.float32
    )
    return (mixed_heads, log_total)


def attend_backward(queries, keys_full, values_full, causal, log_total, mixed_heads):
    scores = score_block(queries, keys_full, causal)
    attn_probs = jnp.exp(scores - log_total)
    probs_low = attn_probs.astype(jnp.bfloat16)
    probs_grad = jnp.einsum(
        "sqhe,skhe->shqk", mixed_heads, values_full, preferred_element_type=jnp.float32
    )
    value_term = jnp.einsum(
        "shqk,sqhe->skhe", probs_low, mixed_heads, preferred_element_type=jnp.float32
    )
    row_dot = jnp.sum(attn_probs * probs_grad, axis=-1, keepdims=True)
    scores_grad = (attn_probs * (probs_grad - row_dot)).astype(jnp.bfloat16)
    query_grad = jnp.einsum(
        "shqk,skhe->sqhe", scores_grad, keys_full, preferred_element_type=jnp.float32
    ) * HD ** (-0.5)
    key_term = jnp.einsum(
        "shqk,sqhe->skhe", scores_grad, queries, preferred_element_type=jnp.float32
    ) * HD ** (-0.5)
    return (query_grad, key_term, value_term)


MESH = pl.DeviceIdType.MESH


def places(chips, groups):
    dp, z = lax.axis_index("dp"), lax.axis_index("seq")
    chip, core = dp // 2, dp % 2
    partner = {"dp": chip * 2 + (1 - core)}
    across = [{"dp": (chip + k) % chips * 2 + core} for k in range(chips)]
    along = [{"seq": (z + k) % groups} for k in range(groups)]
    return chip, core, z, partner, across, along


def greet(partner, across, along):
    barrier = pltpu.get_barrier_semaphore()
    peers = [partner] + across[1:] + along[1:]
    for peer in peers:
        pl.semaphore_signal(barrier, inc=1, device_id=peer, device_id_type=MESH)
    pl.semaphore_wait(barrier, len(peers))


def gather_kernel(
    chips, groups, w_ref, x_ref, c_ref, s_ref, w_all, x_all, c_all, s_all,
    local_sem, w_send, w_recv, p_send, p_recv, z_send, z_recv, sa_send, sa_recv, sp_send, sp_recv,
):
    chip, core, z, partner, across, along = places(chips, groups)
    mine = chip * 2 + core
    local = [
        pltpu.make_async_copy(w_ref, w_all.at[mine], local_sem.at[0]),
        pltpu.make_async_copy(x_ref, x_all.at[z], local_sem.at[1]),
        pltpu.make_async_copy(c_ref, c_all.at[z], local_sem.at[2]),
        pltpu.make_async_copy(s_ref, s_all.at[mine, z], local_sem.at[3]),
    ]
    for copy in local:
        copy.start()
    greet(partner, across, along)

    def remote(source, target, send, recv, peer):
        return pltpu.make_async_remote_copy(
            src_ref=source, dst_ref=target, send_sem=send, recv_sem=recv,
            device_id=peer, device_id_type=MESH,
        )

    smalls, rows, cots, blocks, handed, small_out = [], [], [], [], [], []
    for k in range(1, groups):
        smalls.append(remote(s_ref, s_all.at[mine, z], z_send.at[0, k], z_recv.at[0, k], along[k]))
        smalls[-1].start()
    for k in range(1, chips):
        blocks.append(remote(w_ref, w_all.at[mine], w_send.at[k], w_recv.at[k], across[k]))
        blocks[-1].start()
    handed.append(remote(w_ref, w_all.at[mine], p_send.at[0], p_recv.at[0], partner))
    handed[-1].start()
    for k in range(1, groups):
        rows.append(remote(x_ref, x_all.at[z], z_send.at[1, k], z_recv.at[1, k], along[k]))
        rows[-1].start()
    for k in range(1, groups):
        cots.append(remote(c_ref, c_all.at[z], z_send.at[2, k], z_recv.at[2, k], along[k]))
        cots[-1].start()
    for copy in smalls:
        copy.wait_recv()
    local[3].wait()
    for k in range(1, chips):
        small_out.append(remote(s_all.at[mine], s_all.at[mine], sa_send.at[k], sa_recv.at[k], across[k]))
        small_out[-1].start()
    small_pass = [remote(s_all.at[mine], s_all.at[mine], sp_send.at[0], sp_recv.at[0], partner)]
    small_pass[0].start()
    for k in range(1, chips):
        small_out[k - 1].wait_recv()
        came = (chip + chips - k) % chips * 2 + core
        small_pass.append(remote(s_all.at[came], s_all.at[came], sp_send.at[k], sp_recv.at[k], partner))
        small_pass[-1].start()
    for k in range(1, chips):
        blocks[k - 1].wait_recv()
        came = (chip + chips - k) % chips * 2 + core
        handed.append(remote(w_all.at[came], w_all.at[came], p_send.at[k], p_recv.at[k], partner))
        handed[-1].start()
    for copy in handed + small_pass + rows + cots:
        copy.wait_recv()
    for copy in smalls + small_out + small_pass + blocks + handed + rows + cots:
        copy.wait_send()
    for copy in local[:3]:
        copy.wait()


def gather_all(w, x, c, s, chips, groups):
    any_spec = pl.BlockSpec(memory_space=pl.ANY)
    dma = pltpu.SemaphoreType.DMA
    return pl.pallas_call(
        functools.partial(gather_kernel, chips, groups),
        out_shape=(
            jax.ShapeDtypeStruct((2 * chips,) + w.shape, w.dtype),
            jax.ShapeDtypeStruct((groups,) + x.shape, x.dtype),
            jax.ShapeDtypeStruct((groups,) + c.shape, c.dtype),
            jax.ShapeDtypeStruct((2 * chips, groups) + s.shape, s.dtype),
        ),
        in_specs=[any_spec] * 4,
        out_specs=(any_spec,) * 4,
        scratch_shapes=[
            dma((4,)), dma((chips,)), dma((chips,)), dma((chips,)), dma((chips,)),
            dma((3, groups)), dma((3, groups)),
            dma((chips,)), dma((chips,)), dma((chips,)), dma((chips,)),
        ],
        compiler_params=pltpu.CompilerParams(collective_id=0, has_side_effects=True),
        name="gather_all",
    )(w, x, c, s)


def reduce_kernel(
    chips, groups, g_ref, p_ref, n_ref, v_ref, g_out, p_out, n_out, v_out,
    g_half, g_sum, g_got, p_got, n_got, v_half, v_sum, v_got, v_all, vz_got,
    h_send, h_recv, a_send, a_recv, z_send, z_recv, vh_send, vh_recv, va_send, va_recv, vz_send, vz_recv,
):
    chip, core, z, partner, across, along = places(chips, groups)
    greet(partner, across, along)

    def remote(source, target, send, recv, peer):
        return pltpu.make_async_remote_copy(
            src_ref=source, dst_ref=target, send_sem=send, recv_sem=recv,
            device_id=peer, device_id_type=MESH,
        )

    f32 = jnp.float32
    order = list(range(1, chips)) + [0]
    v_give = remote(v_ref.at[1 - core], v_half, vh_send.at[0], vh_recv.at[0], partner)
    v_give.start()
    halves = {}
    for k in order:
        at = (chip + k) % chips
        halves[k] = remote(g_ref.at[at * 2 + 1 - core], g_half.at[k], h_send.at[k], h_recv.at[k], partner)
        halves[k].start()
    rows = []
    for k in range(1, groups):
        to = (z + k) % groups
        rows.append(remote(p_ref.at[to], p_got.at[k], z_send.at[0, k], z_recv.at[0, k], along[k]))
        rows[-1].start()
        rows.append(remote(n_ref.at[to], n_got.at[k], z_send.at[1, k], z_recv.at[1, k], along[k]))
        rows[-1].start()
    v_give.wait_recv()
    v_sum[...] = v_ref[core] + v_half[...]
    v_across = []
    for k in range(1, chips):
        at = (chip + k) % chips
        v_across.append(remote(v_sum.at[at], v_got.at[k], va_send.at[k], va_recv.at[k], across[k]))
        v_across[-1].start()
    sums = []
    for k in order:
        at = (chip + k) % chips
        halves[k].wait_recv()
        both = g_ref[at * 2 + core].astype(f32) + g_half[k].astype(f32)
        if k > 0:
            g_sum[k] = both.astype(g_sum.dtype)
            sums.append(remote(g_sum.at[k], g_got.at[k], a_send.at[k], a_recv.at[k], across[k]))
            sums[-1].start()
        else:
            g_out[...] = both
    for copy in v_across:
        copy.wait_recv()
    total = v_sum[chip]
    for k in range(1, chips):
        total = total + v_got[k]
    v_all[...] = total
    v_along = []
    for k in range(1, groups):
        to = (z + k) % groups
        v_along.append(remote(v_all.at[to], vz_got.at[k], vz_send.at[k], vz_recv.at[k], along[k]))
        v_along[-1].start()
    for copy in rows:
        copy.wait_recv()
    p_out[...] = p_ref[z].astype(f32)
    n_out[...] = n_ref[z].astype(f32)
    for k in range(1, groups):
        p_out[...] += p_got[k].astype(f32)
        n_out[...] += n_got[k].astype(f32)
    for copy in v_along:
        copy.wait_recv()
    total = v_all[z]
    for k in range(1, groups):
        total = total + vz_got[k]
    v_out[...] = total
    for k in range(1, chips):
        sums[k - 1].wait_recv()
        g_out[...] += g_got[k].astype(f32)
    for copy in [v_give] + list(halves.values()) + rows + v_across + sums + v_along:
        copy.wait_send()


def reduce_all(g, p, n, v, chips, groups):
    vm = pl.BlockSpec(memory_space=pltpu.VMEM)
    dma = pltpu.SemaphoreType.DMA
    block, rows, small = g.shape[1:], p.shape[1:], v.shape[3:]
    f32 = jnp.float32
    return pl.pallas_call(
        functools.partial(reduce_kernel, chips, groups),
        out_shape=(
            jax.ShapeDtypeStruct(block, f32),
            jax.ShapeDtypeStruct(rows, f32),
            jax.ShapeDtypeStruct(rows, f32),
            jax.ShapeDtypeStruct(small, f32),
        ),
        in_specs=[vm] * 4,
        out_specs=(vm,) * 4,
        scratch_shapes=[
            pltpu.VMEM((chips,) + block, g.dtype),
            pltpu.VMEM((chips,) + block, g.dtype),
            pltpu.VMEM((chips,) + block, g.dtype),
            pltpu.VMEM((groups,) + rows, p.dtype),
            pltpu.VMEM((groups,) + rows, p.dtype),
            pltpu.VMEM((chips, groups) + small, f32),
            pltpu.VMEM((chips, groups) + small, f32),
            pltpu.VMEM((chips, groups) + small, f32),
            pltpu.VMEM((groups,) + small, f32),
            pltpu.VMEM((groups,) + small, f32),
            dma((chips,)), dma((chips,)), dma((chips,)), dma((chips,)),
            dma((2, groups)), dma((2, groups)),
            dma((1,)), dma((1,)), dma((chips,)), dma((chips,)), dma((groups,)), dma((groups,)),
        ],
        compiler_params=pltpu.CompilerParams(
            collective_id=1, has_side_effects=True, vmem_limit_bytes=48 * 2**20
        ),
        name="reduce_all",
    )(g, p, n, v)


def body(hidden_in, out_grad, norm_params, biases, attn_in, attn_out, mlp_up, mlp_down):
    local_len = hidden_in.shape[1]
    groups, devices = lax.axis_size("seq"), lax.axis_size("dp")
    chips = devices // 2
    z = lax.axis_index("seq")
    f32, bf16 = jnp.float32, jnp.bfloat16
    heads, col_width, ff_width = H // groups, 3 * D // groups, FF // groups
    out_width = D // groups
    norm_size, bias_size = norm_params.shape[0], biases.shape[0]
    small_size = norm_size + bias_size
    small_pad = -small_size % 128

    packed = jnp.concatenate([attn_in, attn_out.T, mlp_up, mlp_down.T], axis=1)
    small = jnp.pad(jnp.concatenate([norm_params, biases]), (0, small_pad))
    small = jnp.broadcast_to(small[None, :], (16, small_size + small_pad))
    w_all, x_all, c_all, s_all = gather_all(packed, hidden_in[0], out_grad[0], small, chips, groups)
    tok_len = local_len * groups
    w = w_all.reshape(D, -1)
    w_in = w[:, :col_width]
    w_out_t = w[:, col_width : col_width + out_width]
    w_up = w[:, col_width + out_width : col_width + out_width + ff_width]
    w_down_t = w[:, col_width + out_width + ff_width :]
    small_rows = s_all[:, :, 0, :].astype(f32)
    norm_vec = small_rows[:, :, :norm_size].reshape(4, D)
    bias_vec = small_rows[:, :, norm_size:small_size].reshape(-1)
    in_bias = lax.dynamic_slice_in_dim(bias_vec, z * col_width, col_width)
    up_bias = lax.dynamic_slice_in_dim(bias_vec, 3 * D + z * ff_width, ff_width)
    out_bias = bias_vec[3 * D + FF :]

    cot = c_all.reshape(tok_len, D)
    inputs = x_all.reshape(tok_len, D).astype(f32)
    average = jnp.mean(inputs, axis=-1, keepdims=True)
    centered = inputs - average
    inv_std = lax.rsqrt(jnp.mean(centered * centered, axis=-1, keepdims=True) + norm_eps)
    normed = centered * inv_std
    attn_rows = (normed * norm_vec[0] + norm_vec[1]).astype(bf16)
    mlp_rows = (normed * norm_vec[2] + norm_vec[3]).astype(bf16)

    def mul(a, b, ca, cb):
        return lax.dot_general(a, b, (((ca,), (cb,)), ((), ())), preferred_element_type=f32)

    triple = mul(attn_rows, w_in, 1, 0) + in_bias
    split = triple.reshape(1, tok_len, heads, 3, HD)
    query_pos = jnp.arange(tok_len, dtype=jnp.int32)
    cosine_table, sine_table = rotary_tables(query_pos.astype(f32))
    queries = rotate(split[:, :, :, 0], cosine_table, sine_table).astype(bf16)
    key_rows = rotate(split[:, :, :, 1], cosine_table, sine_table).astype(bf16)
    value_rows = split[:, :, :, 2].astype(bf16)
    causal = query_pos[:, None] >= query_pos[None, :]
    mixed_heads, log_total = attend_forward(queries, key_rows, value_rows, causal)
    mixed_rows = mixed_heads.reshape(tok_len, heads * HD).astype(bf16)
    hidden = mul(mlp_rows, w_up, 1, 0) + up_bias
    activated = gelu(hidden).astype(bf16)
    branch = mul(mixed_rows, w_out_t, 1, 1) + mul(activated, w_down_t, 1, 1)

    down_term = mul(cot, activated, 0, 0)
    hidden_grad = (mul(cot, w_down_t, 1, 0) * gelu_slope(hidden)).astype(bf16)
    up_term = mul(mlp_rows, hidden_grad, 0, 0)
    up_sum = jnp.sum(hidden_grad.astype(f32), axis=0)
    mlp_grad = mul(hidden_grad, w_up, 1, 1)
    mixed_grad = mul(cot, w_out_t, 1, 0).astype(bf16)
    out_term = mul(cot, mixed_rows, 0, 0)
    query_grad, key_grad, value_grad = attend_backward(
        queries, key_rows, value_rows, causal, log_total, mixed_grad.reshape(1, tok_len, heads, HD)
    )
    triple_grad = (
        jnp.stack(
            [
                rotate_back(query_grad, cosine_table, sine_table),
                rotate_back(key_grad, cosine_table, sine_table),
                value_grad,
            ],
            axis=3,
        )
        .reshape(tok_len, col_width)
        .astype(bf16)
    )
    in_term = mul(attn_rows, triple_grad, 0, 0)
    triple_sum = jnp.sum(triple_grad.astype(f32), axis=0)
    attn_grad = mul(triple_grad, w_in, 1, 1)
    normed_grad = attn_grad * norm_vec[0] + mlp_grad * norm_vec[2]

    norm_term = jnp.stack(
        [
            jnp.sum(attn_grad * normed, axis=0),
            jnp.sum(attn_grad, axis=0),
            jnp.sum(mlp_grad * normed, axis=0),
            jnp.sum(mlp_grad, axis=0),
        ]
    ).reshape(devices, groups, norm_size)
    cot_own = out_grad[0].astype(f32)
    bias_term = jnp.zeros((4 * D + FF,), f32)
    bias_term = lax.dynamic_update_slice(bias_term, triple_sum, (z * col_width,))
    bias_term = lax.dynamic_update_slice(bias_term, up_sum, (3 * D + z * ff_width,))
    bias_term = lax.dynamic_update_slice(bias_term, jnp.sum(cot_own, axis=0), (jnp.int32(3 * D + FF),))
    small_pad = -small_size % 1024
    v = jnp.concatenate([norm_term, bias_term.reshape(devices, groups, bias_size)], axis=2)
    v = jnp.pad(v, ((0, 0), (0, 0), (0, small_pad)))
    v = v.reshape(chips, 2, groups, (small_size + small_pad) // 128, 128).transpose(1, 0, 2, 3, 4)

    g = jnp.concatenate([in_term, out_term, up_term, down_term], axis=1).astype(bf16)
    g = g.reshape(devices, D // devices, -1)
    g_sum, branch_sum, normed_grad, v_sum = reduce_all(
        g,
        branch.astype(bf16).reshape(groups, local_len, D),
        normed_grad.astype(bf16).reshape(groups, local_len, D),
        v,
        chips,
        groups,
    )
    own = hidden_in[0].astype(f32)
    layer_out = (own + branch_sum + out_bias).astype(bf16)[None]
    own_average = jnp.mean(own, axis=-1, keepdims=True)
    own_centered = own - own_average
    own_std = lax.rsqrt(jnp.mean(own_centered * own_centered, axis=-1, keepdims=True) + norm_eps)
    own_normed = own_centered * own_std
    input_term = own_std * (
        normed_grad
        - jnp.mean(normed_grad, axis=-1, keepdims=True)
        - own_normed * jnp.mean(normed_grad * own_normed, axis=-1, keepdims=True)
    )
    grad_input = (cot_own + input_term).astype(bf16)[None]
    flat = v_sum.reshape(-1)
    return (
        layer_out,
        grad_input,
        flat[:norm_size],
        flat[norm_size:small_size],
        g_sum[:, :col_width],
        g_sum[:, col_width : col_width + out_width].T,
        g_sum[:, col_width + out_width : col_width + out_width + ff_width],
        g_sum[:, col_width + out_width + ff_width :].T,
    )


def solution(mesh):
    in_specs = (
        P("dp", "seq", None),
        P("dp", "seq", None),
        P(("dp", "seq")),
        P(("dp", "seq")),
        P("dp", "seq"),
        P("seq", "dp"),
        P("dp", "seq"),
        P("seq", "dp"),
    )
    out_specs = (
        P("dp", "seq", None),
        P("dp", "seq", None),
        P(("dp", "seq")),
        P(("dp", "seq")),
        P("dp", "seq"),
        P("seq", "dp"),
        P("dp", "seq"),
        P("seq", "dp"),
    )
    return jax.shard_map(body, mesh=mesh, in_specs=in_specs, out_specs=out_specs, check_vma=False)
```

```python
import functools
import math

import jax
import jax.numpy as jnp
import numpy as np
from jax import lax
from jax.experimental import pallas as pl
from jax.experimental.pallas import tpu as pltpu
from jax.sharding import PartitionSpec as P

D = 1024
H = 16
HD = 64
FF = 4096
ROT = 16
LANES = 128

norm_eps = 1e-05
masked_score = -1e30
MESH = pl.DeviceIdType.MESH
f32, bf16 = jnp.float32, jnp.bfloat16


def rotary_tables(tok_len):
    half = ROT // 2
    frequency = np.power(np.float32(10000.0), np.float32(-2.0) * np.arange(half, dtype=np.float32) / np.float32(ROT))
    angles = np.arange(tok_len, dtype=np.float32)[:, None] * frequency.astype(np.float32)[None, :]
    cosine, sine = np.cos(angles.astype(np.float64)), np.sin(angles.astype(np.float64))
    keep = np.ones((tok_len, 2, 3, HD), np.float32)
    right = np.zeros((tok_len, 2, 3, HD), np.float32)
    left = np.zeros((tok_len, 2, 3, HD), np.float32)
    for part in range(2):
        keep[:, :, part, :half] = cosine[:, None]
        keep[:, :, part, half:ROT] = cosine[:, None]
        right[:, :, part, :half] = -sine[:, None]
        left[:, :, part, half:ROT] = sine[:, None]
    return [jnp.asarray(table.reshape(tok_len, 6 * HD)) for table in (keep, right, left)]


def mul(a, b, ca, cb):
    return lax.dot_general(a, b, (((ca,), (cb,)), ((), ())), preferred_element_type=f32)


def layer_kernel(
    chips, groups,
    w_ref, x_ref, c_ref, s_ref, keep_ref, right_ref, left_ref,
    lay_ref, gin_ref, g_out, v_out,
    w_all, x_all, c_all, s_all, normed, rows_a, rows_m, turned_a, turned_m, turned_c,
    q_s, k_s, v_s, probs, mixed_s, both_rows, slope, hid_grad, mg_s, dq_s, dk_s, dv_s, low_p, low_ds, tg,
    p_out, p_got, n_out, n_got, g, g_half, g_sum, g_got, v_mine, v_half, v_sum, v_got, v_all, v_last,
    local_sem, w_send, w_recv, h_send, h_recv, s_send, s_recv, z_send, z_recv,
    gh_send, gh_recv, ga_send, ga_recv, v_send, v_recv,
):
    length, tok_len = x_ref.shape[0], x_all.shape[0]
    depth = w_ref.shape[0]
    heads = H // groups
    in_width, out_width, up_width = 3 * D // groups, D // groups, FF // groups
    at_up, at_out = in_width, in_width + up_width
    at_down, width = at_out + out_width, at_out + out_width + up_width
    pieces = [(0, in_width), (at_up, up_width), (at_out, out_width + up_width)]
    norm_size, bias_size = 4 * D // (2 * chips * groups), (4 * D + FF) // (2 * chips * groups)

    dp, z = lax.axis_index("dp"), lax.axis_index("seq")
    chip, core = dp // 2, dp % 2
    partner = {"dp": chip * 2 + (1 - core)}
    across = [{"dp": (chip + k) % chips * 2 + core} for k in range(chips)]
    along = [{"seq": (z + k) % groups} for k in range(groups)]

    def block(at, size):
        return pl.ds(pl.multiple_of(at * size, size), size)

    def remote(source, target, send, recv, at, peer):
        return pltpu.make_async_remote_copy(
            src_ref=source, dst_ref=target, send_sem=send.at[at], recv_sem=recv.at[at],
            device_id=peer, device_id_type=MESH,
        )

    started = []

    def send(*args):
        copy = remote(*args)
        copy.start()
        started.append(copy)
        return copy

    own_rows, own_toks = block(dp, depth), block(z, length)
    local = [
        pltpu.make_async_copy(w_ref, w_all.at[own_rows], local_sem.at[0]),
        pltpu.make_async_copy(x_ref, x_all.at[own_toks], local_sem.at[1]),
        pltpu.make_async_copy(c_ref, c_all.at[own_toks], local_sem.at[2]),
        pltpu.make_async_copy(s_ref, s_all.at[dp, z], local_sem.at[3]),
    ]
    for copy in local:
        copy.start()
    barrier = pltpu.get_barrier_semaphore()
    peers = [partner] + across[1:] + along[1:]
    for peer in peers:
        pl.semaphore_signal(barrier, inc=1, device_id=peer, device_id_type=MESH)
    pl.semaphore_wait(barrier, len(peers))

    smalls = [send(s_ref, s_all.at[dp, z], z_send, z_recv, (0, k), along[k]) for k in range(1, groups)]
    weights, handed = {}, {}

    def send_piece(at):
        cols = pl.ds(*pieces[at])
        for k in range(1, chips):
            weights[at, k] = send(
                w_ref.at[:, cols], w_all.at[own_rows, cols], w_send, w_recv, (at, k), across[k]
            )
        handed[at] = [
            send(w_ref.at[:, cols], w_all.at[own_rows, cols], h_send, h_recv, (at, 0), partner)
        ]

    def take_piece(at):
        cols = pl.ds(*pieces[at])
        for k in range(1, chips):
            weights[at, k].wait_recv()
            came = block((chip + chips - k) % chips * 2 + core, depth)
            handed[at].append(
                send(w_all.at[came, cols], w_all.at[came, cols], h_send, h_recv, (at, k), partner)
            )
        for copy in handed[at]:
            copy.wait_recv()

    send_piece(0)
    x_moves = [send(x_ref, x_all.at[own_toks], z_send, z_recv, (1, k), along[k]) for k in range(1, groups)]
    send_piece(1)
    send_piece(2)
    c_moves = [send(c_ref, c_all.at[own_toks], z_send, z_recv, (2, k), along[k]) for k in range(1, groups)]

    local[3].wait()
    for copy in smalls:
        copy.wait_recv()
    out = [send(s_all.at[dp], s_all.at[dp], s_send, s_recv, (0, k), across[k]) for k in range(1, chips)]
    over = [send(s_all.at[dp], s_all.at[dp], s_send, s_recv, (1, 0), partner)]
    for k in range(1, chips):
        out[k - 1].wait_recv()
        came = (chip + chips - k) % chips * 2 + core
        over.append(send(s_all.at[came], s_all.at[came], s_send, s_recv, (1, k), partner))
    for copy in over:
        copy.wait_recv()
    for copy in x_moves:
        copy.wait_recv()
    local[1].wait()

    def owners(size, base, step, row, first):
        per, share = max(size // LANES, 1), max(LANES // size, 1)
        at = base // per * share + z * (step // per * share) + row // per * share
        return [((at + j) // groups, (at + j) % groups, first + row % per) for j in range(share)]

    def small_vector(size, base, step, count, first):
        parts = []
        for row in range(count):
            total = None
            for d_at, z_at, line in owners(size, base, step, row, first):
                value = s_all[d_at, z_at][line : line + 1, :]
                total = value if total is None else total + value
            parts.append(total)
        return jnp.concatenate(parts, axis=1)

    norm_vec = [small_vector(norm_size, r * (D // LANES), 0, D // LANES, 0) for r in range(4)]

    def normalise(values):
        centered = values - jnp.mean(values, axis=-1, keepdims=True)
        inv_std = lax.rsqrt(jnp.mean(centered * centered, axis=-1, keepdims=True) + norm_eps)
        return centered * inv_std, inv_std

    def norm_step(i, carry):
        at = block(i, length)
        part, _ = normalise(x_all[at, :].astype(f32))
        normed[at, :] = part
        a_part = part * norm_vec[0] + norm_vec[1]
        m_part = part * norm_vec[2] + norm_vec[3]
        rows_a[at, :] = a_part.astype(bf16)
        rows_m[at, :] = m_part.astype(bf16)
        turned_a[:, at] = a_part.T.astype(bf16)
        turned_m[:, at] = m_part.T.astype(bf16)
        return carry

    lax.fori_loop(0, groups, norm_step, 0)

    in_bias = small_vector(bias_size, 0, in_width // LANES, in_width // LANES, 1)
    local[0].wait()
    take_piece(0)
    pair = 6 * HD

    def turn(values, sign):
        return (
            values * keep_ref[...]
            + sign * (pltpu.roll(values, pair - ROT // 2, 1) * right_ref[...])
            + sign * (pltpu.roll(values, ROT // 2, 1) * left_ref[...])
        )

    for two in range(heads // 2):
        cols = slice(two * pair, (two + 1) * pair)
        triple = mul(rows_a[...], w_all[:, cols], 1, 0) + in_bias[:, cols]
        triple = turn(triple, 1.0)
        for j in range(2):
            h = two * 2 + j
            q_s[h] = triple[:, j * 192 : j * 192 + 64].astype(bf16)
            k_s[h] = triple[:, j * 192 + 64 : j * 192 + 128].astype(bf16)
            v_s[h] = triple[:, j * 192 + 128 : j * 192 + 192].astype(bf16)

    step_rows = 128
    scale = HD ** (-0.5)

    def attend(h):
        for b in range(tok_len // step_rows):
            at, seen = slice(b * step_rows, (b + 1) * step_rows), (b + 1) * step_rows
            scores = mul(q_s[h, at, :], k_s[h, :seen, :], 1, 1) * scale
            q_pos = lax.broadcasted_iota(jnp.int32, scores.shape, 0) + b * step_rows
            k_pos = lax.broadcasted_iota(jnp.int32, scores.shape, 1)
            scores = jnp.where(q_pos >= k_pos, scores, masked_score)
            row_max = jnp.max(scores, axis=-1, keepdims=True)
            powers = jnp.exp(scores - row_max)
            part = powers * (1.0 / jnp.sum(powers, axis=-1, keepdims=True))
            probs[h, at, :seen] = part
            mixed_s[h, at, :] = mul(part.astype(bf16), v_s[h, :seen, :], 1, 0)

    for h in range(heads):
        attend(h)
    both_rows[:, :out_width] = jnp.concatenate([mixed_s[h] for h in range(heads)], axis=1).astype(bf16)

    up_bias = small_vector(bias_size, 3 * D // LANES, up_width // LANES, up_width // LANES, 1)
    take_piece(1)
    wide = 256
    for j in range(up_width // wide):
        cols = slice(j * wide, (j + 1) * wide)
        up_cols = slice(at_up + j * wide, at_up + (j + 1) * wide)
        hidden = mul(rows_m[...], w_all[:, up_cols], 1, 0) + up_bias[:, cols]
        half = 0.5 * (1.0 + lax.erf(hidden * (1.0 / math.sqrt(2.0))))
        both_rows[:, out_width + j * wide : out_width + (j + 1) * wide] = (hidden * half).astype(bf16)
        slope[:, cols] = half + hidden * jnp.exp(-0.5 * hidden * hidden) * (1.0 / math.sqrt(2.0 * math.pi))

    take_piece(2)
    p_moves = []
    for k in list(range(1, groups)) + [0]:
        at = block((z + k) % groups, length)
        part = mul(both_rows[at, :], w_all[:, at_out:], 1, 1)
        p_out[k] = part.astype(bf16)
        if k > 0:
            p_moves.append(send(p_out.at[k], p_got.at[k], z_send, z_recv, (3, k), along[k]))

    for copy in c_moves:
        copy.wait_recv()
    local[2].wait()

    def turn_cot(i, carry):
        at = block(i, length)
        turned_c[:, at] = c_all[at, :].astype(f32).T.astype(bf16)
        return carry

    lax.fori_loop(0, groups, turn_cot, 0)
    halves, sums = {}, []
    order = list(range(1, chips)) + [0]

    def give(at):
        cols = pl.ds(*pieces[at])
        for k in order:
            rows = block((chip + k) % chips * 2 + 1 - core, depth)
            halves[at, k] = send(
                g.at[rows, cols], g_half.at[k, :, cols], gh_send, gh_recv, (at, k), partner
            )

    def add(at):
        cols = pl.ds(*pieces[at])
        for k in order:
            rows = block((chip + k) % chips * 2 + core, depth)
            halves[at, k].wait_recv()
            both = g[rows, cols].astype(f32) + g_half[k, :, cols].astype(f32)
            if k > 0:
                g_sum[k, :, cols] = both.astype(bf16)
                sums.append(
                    send(g_sum.at[k, :, cols], g_got.at[k, :, cols], ga_send, ga_recv, (at, k), across[k])
                )
            else:
                g_out[:, cols] = both

    for j in range((out_width + up_width) // wide):
        cols = slice(j * wide, (j + 1) * wide)
        g[:, at_out + j * wide : at_out + (j + 1) * wide] = mul(turned_c[...], both_rows[:, cols], 1, 0).astype(bf16)
    give(2)

    up_sums = []
    for j in range(up_width // wide):
        cols = slice(j * wide, (j + 1) * wide)
        part = mul(c_all[...], w_all[:, at_down + j * wide : at_down + (j + 1) * wide], 1, 0) * slope[:, cols]
        part = part.astype(bf16)
        hid_grad[:, cols] = part
        up_sums.append(jnp.sum(part.astype(f32), axis=0, keepdims=True))
    add(2)
    for j in range(up_width // wide):
        cols = slice(j * wide, (j + 1) * wide)
        g[:, at_up + j * wide : at_up + (j + 1) * wide] = mul(turned_m[...], hid_grad[:, cols], 1, 0).astype(bf16)
    give(1)

    mixed_grad = mul(c_all[...], w_all[:, at_out:at_down], 1, 0).astype(bf16)
    for h in range(heads):
        mg_s[h] = mixed_grad[:, h * HD : (h + 1) * HD]
    add(1)

    def attend_back(h):
        for b in range(tok_len // step_rows):
            at, seen = slice(b * step_rows, (b + 1) * step_rows), (b + 1) * step_rows
            part, m_grad = probs[h, at, :seen], mg_s[h, at, :]
            p_grad = mul(m_grad, v_s[h, :seen, :], 1, 1)
            row_dot = jnp.sum(part * p_grad, axis=-1, keepdims=True)
            s_grad = (part * (p_grad - row_dot)).astype(bf16)
            dq_s[h, at, :] = mul(s_grad, k_s[h, :seen, :], 1, 0) * scale
            low_p[at, :seen] = part.astype(bf16)
            low_ds[at, :seen] = s_grad
        for b in range(tok_len // step_rows):
            at, late = slice(b * step_rows, (b + 1) * step_rows), slice(b * step_rows, tok_len)
            dk_s[h, at, :] = mul(low_ds[late, at], q_s[h, late, :], 0, 0) * scale
            dv_s[h, at, :] = mul(low_p[late, at], mg_s[h, late, :], 0, 0)

    for h in range(heads):
        attend_back(h)
    in_sums = []
    for two in range(heads // 2):
        joined = []
        for h in (two * 2, two * 2 + 1):
            joined += [dq_s[h], dk_s[h], dv_s[h]]
        part = turn(jnp.concatenate(joined, axis=1), -1.0).astype(bf16)
        tg[:, two * pair : (two + 1) * pair] = part
        in_sums.append(jnp.sum(part.astype(f32), axis=0, keepdims=True))

    norm_sums = None
    n_moves = []
    for k in list(range(1, groups)) + [0]:
        at = block((z + k) % groups, length)
        a_grad = mul(tg[at, :], w_all[:, :in_width], 1, 1)
        m_grad = mul(hid_grad[at, :], w_all[:, at_up:at_out], 1, 1)
        n_out[k] = (a_grad * norm_vec[0] + m_grad * norm_vec[2]).astype(bf16)
        if k > 0:
            n_moves.append(send(n_out.at[k], n_got.at[k], z_send, z_recv, (4, k), along[k]))
        part = normed[at, :]
        terms = [a_grad * part, a_grad, m_grad * part, m_grad]
        terms = [jnp.sum(term, axis=0, keepdims=True) for term in terms]
        norm_sums = terms if norm_sums is None else [a + b for a, b in zip(norm_sums, terms)]

    for j in range(in_width // wide):
        cols = slice(j * wide, (j + 1) * wide)
        g[:, cols] = mul(turned_a[...], tg[:, cols], 1, 0).astype(bf16)
    give(0)

    v_mine[...] = jnp.zeros_like(v_mine)

    def place(vector, size, base, step, first):
        for row in range(vector.shape[1] // LANES):
            for d_at, z_at, line in owners(size, base, step, row, first):
                v_mine[d_at, z_at, line : line + 1, :] = vector[:, row * LANES : (row + 1) * LANES]

    for r in range(4):
        place(norm_sums[r], norm_size, r * (D // LANES), 0, 0)
    place(jnp.concatenate(in_sums, axis=1), bias_size, 0, in_width // LANES, 1)
    place(jnp.concatenate(up_sums, axis=1), bias_size, 3 * D // LANES, up_width // LANES, 1)
    cot_own = c_ref[...].astype(f32)
    place(jnp.sum(cot_own, axis=0, keepdims=True), bias_size, (3 * D + FF) // LANES, 0, 1)
    v_give = [
        send(v_mine.at[(chip + k) % chips * 2 + 1 - core], v_half.at[k], v_send, v_recv, (0, k), partner)
        for k in range(chips)
    ]
    add(0)
    v_across = []
    for k in order:
        v_give[k].wait_recv()
        v_sum[k] = v_mine[(chip + k) % chips * 2 + core] + v_half[k]
        if k > 0:
            v_across.append(send(v_sum.at[k], v_got.at[k], v_send, v_recv, (1, k), across[k]))

    for copy in p_moves:
        copy.wait_recv()
    out_bias = small_vector(bias_size, (3 * D + FF) // LANES, 0, D // LANES, 1)
    own = x_ref[...].astype(f32)
    total = p_out[0].astype(f32)
    for k in range(1, groups):
        total = total + p_got[k].astype(f32)
    lay_ref[...] = (own + total + out_bias).astype(bf16)

    total = v_sum[0]
    for copy in v_across:
        copy.wait_recv()
    for k in range(1, chips):
        total = total + v_got[k]
    v_all[...] = total
    v_along = [
        send(v_all.at[(z + k) % groups], v_last.at[k], z_send, z_recv, (5, k), along[k])
        for k in range(1, groups)
    ]

    for copy in n_moves:
        copy.wait_recv()
    own_normed, own_std = normalise(own)
    total = n_out[0].astype(f32)
    for k in range(1, groups):
        total = total + n_got[k].astype(f32)
    term = own_std * (
        total
        - jnp.mean(total, axis=-1, keepdims=True)
        - own_normed * jnp.mean(total * own_normed, axis=-1, keepdims=True)
    )
    gin_ref[...] = (cot_own + term).astype(bf16)

    for copy in v_along:
        copy.wait_recv()
    total = v_all[z]
    for k in range(1, groups):
        total = total + v_last[k]
    v_out[...] = total

    for copy in sums:
        copy.wait_recv()
    total = g_out[...]
    for k in range(1, chips):
        total = total + g_got[k].astype(f32)
    g_out[...] = total
    for copy in started:
        copy.wait_send()


def layer(w, x, c, s, tables, chips, groups):
    vm = pl.BlockSpec(memory_space=pltpu.VMEM)
    dma = pltpu.SemaphoreType.DMA
    length, depth, width = x.shape[0], w.shape[0], w.shape[1]
    tok_len, devices, heads = length * groups, 2 * chips, H // groups
    up_width, in_width = FF // groups, 3 * D // groups
    shape, rows, head = (tok_len, D), (groups, length, D), (heads, tok_len, HD)
    tile = (8, LANES)
    buffers = [
        ((D, width), bf16), (shape, bf16), (shape, bf16), ((devices, groups) + tile, f32),
        (shape, f32), (shape, bf16), (shape, bf16),
        ((D, tok_len), bf16), ((D, tok_len), bf16), ((D, tok_len), bf16),
        (head, bf16), (head, bf16), (head, bf16), ((heads, tok_len, tok_len), f32), (head, f32),
        ((tok_len, heads * HD + up_width), bf16), ((tok_len, up_width), f32),
        ((tok_len, up_width), bf16), (head, bf16), (head, f32), (head, f32), (head, f32),
        ((tok_len, tok_len), bf16), ((tok_len, tok_len), bf16),
        ((tok_len, in_width), bf16),
        (rows, bf16), (rows, bf16), (rows, bf16), (rows, bf16),
        ((D, width), bf16), ((chips, depth, width), bf16), ((chips, depth, width), bf16),
        ((chips, depth, width), bf16),
        ((devices, groups) + tile, f32), ((chips, groups) + tile, f32), ((chips, groups) + tile, f32),
        ((chips, groups) + tile, f32), ((groups,) + tile, f32), ((groups,) + tile, f32),
    ]
    sems = [(4,)] + [(3, chips)] * 4 + [(2, chips)] * 2 + [(6, groups)] * 2 + [(3, chips)] * 4 + [(2, chips)] * 2
    return pl.pallas_call(
        functools.partial(layer_kernel, chips, groups),
        out_shape=(
            jax.ShapeDtypeStruct(x.shape, bf16),
            jax.ShapeDtypeStruct(x.shape, bf16),
            jax.ShapeDtypeStruct(w.shape, f32),
            jax.ShapeDtypeStruct(tile, f32),
        ),
        in_specs=[vm] * 7,
        out_specs=(vm,) * 4,
        scratch_shapes=[pltpu.VMEM(*buffer) for buffer in buffers] + [dma(sem) for sem in sems],
        compiler_params=pltpu.CompilerParams(
            collective_id=0, has_side_effects=True, vmem_limit_bytes=60 * 2**20
        ),
        name="layer",
    )(w, x, c, s, *tables)


def body(hidden_in, out_grad, norm_params, biases, attn_in, attn_out, mlp_up, mlp_down):
    groups, devices = lax.axis_size("seq"), lax.axis_size("dp")
    chips = devices // 2
    length = hidden_in.shape[1]
    in_width, out_width, up_width = attn_in.shape[1], attn_out.shape[0], mlp_up.shape[1]
    norm_size, bias_size = norm_params.shape[0], biases.shape[0]
    flat = lax.axis_index("dp") * groups + lax.axis_index("seq")

    def tile_rows(values):
        size = values.shape[0]
        if size >= LANES:
            return values.reshape(size // LANES, LANES)
        offset = flat % (LANES // size) * size
        return lax.dynamic_update_slice(jnp.zeros((LANES,), values.dtype), values, (offset,))[None]

    def from_rows(rows, size):
        if size >= LANES:
            return rows.reshape(size)
        return lax.dynamic_slice(rows.reshape(LANES), (flat % (LANES // size) * size,), (size,))

    small = jnp.concatenate([tile_rows(norm_params.astype(f32)), tile_rows(biases.astype(f32))], axis=0)
    norm_lines, lines = max(norm_size // LANES, 1), small.shape[0]
    small = jnp.pad(small, ((0, 8 - lines), (0, 0)))
    packed = jnp.concatenate([attn_in, mlp_up, attn_out.T, mlp_down.T], axis=1)
    layer_out, grad_input, grads, sums = layer(
        packed, hidden_in[0], out_grad[0], small, rotary_tables(length * groups), chips, groups
    )
    at_out = in_width + up_width
    return (
        layer_out[None],
        grad_input[None],
        from_rows(sums[:norm_lines], norm_size),
        from_rows(sums[norm_lines:lines], bias_size),
        grads[:, :in_width],
        grads[:, at_out : at_out + out_width].T,
        grads[:, in_width:at_out],
        grads[:, at_out + out_width :].T,
    )


def solution(mesh):
    in_specs = (
        P("dp", "seq", None),
        P("dp", "seq", None),
        P(("dp", "seq")),
        P(("dp", "seq")),
        P("dp", "seq"),
        P("seq", "dp"),
        P("dp", "seq"),
        P("seq", "dp"),
    )
    out_specs = (
        P("dp", "seq", None),
        P("dp", "seq", None),
        P(("dp", "seq")),
        P(("dp", "seq")),
        P("dp", "seq"),
        P("seq", "dp"),
        P("dp", "seq"),
        P("seq", "dp"),
    )
    return jax.shard_map(body, mesh=mesh, in_specs=in_specs, out_specs=out_specs, check_vma=False)
```

```python
import functools
import math

import jax
import jax.numpy as jnp
import numpy as np
from jax import lax
from jax.experimental import pallas as pl
from jax.experimental.pallas import tpu as pltpu
from jax.sharding import PartitionSpec as P

D = 1024
H = 16
HD = 64
FF = 4096
ROT = 16
LANES = 128

norm_eps = 1e-05
masked_score = -1e30
MESH = pl.DeviceIdType.MESH
f32, bf16 = jnp.float32, jnp.bfloat16


def rotary_tables(tok_len):
    half = ROT // 2
    frequency = np.power(np.float32(10000.0), np.float32(-2.0) * np.arange(half, dtype=np.float32) / np.float32(ROT))
    angles = np.arange(tok_len, dtype=np.float32)[:, None] * frequency.astype(np.float32)[None, :]
    cosine, sine = np.cos(angles.astype(np.float64)), np.sin(angles.astype(np.float64))
    keep = np.ones((tok_len, 2, 3, HD), np.float32)
    right = np.zeros((tok_len, 2, 3, HD), np.float32)
    left = np.zeros((tok_len, 2, 3, HD), np.float32)
    for part in range(2):
        keep[:, :, part, :half] = cosine[:, None]
        keep[:, :, part, half:ROT] = cosine[:, None]
        right[:, :, part, :half] = -sine[:, None]
        left[:, :, part, half:ROT] = sine[:, None]
    return [jnp.asarray(table.reshape(tok_len, 6 * HD)) for table in (keep, right, left)]


def mul(a, b, ca, cb):
    return lax.dot_general(a, b, (((ca,), (cb,)), ((), ())), preferred_element_type=f32)


def layer_kernel(
    chips, groups,
    win_ref, wout_ref, wup_ref, wdown_ref, x_ref, c_ref, nrm_ref, bias_ref, keep_ref, right_ref, left_ref,
    lay_ref, gin_ref, gi_ref, go_ref, gu_ref, gd_ref, v_out,
    w_all, x_all, c_all, s_all, normed, rows_a, rows_m, turned_a, turned_m, turned_c,
    q_s, k_s, v_s, probs, mixed_s, both_rows, slope, hid_grad, mg_s, dq_s, dk_s, dv_s, low_p, low_ds, tg,
    p_out, p_got, n_out, n_got, g, g_half, g_sum, g_got, v_mine, v_half, v_sum, v_got, v_all, v_last,
    g_out, s_mine, w_send, w_recv, h_send, h_recv, s_send, s_recv, z_send, z_recv, x_send, x_recv,
    gh_send, gh_recv, ga_send, ga_recv, v_send, v_recv,
):
    length, tok_len = x_ref.shape[0], x_all.shape[0]
    depth = win_ref.shape[0]
    heads = H // groups
    in_width, out_width, up_width = 3 * D // groups, D // groups, FF // groups
    at_up, at_out = in_width, in_width + up_width
    at_down, width = at_out + out_width, at_out + out_width + up_width
    pieces = [(0, in_width), (at_up, up_width), (at_out, out_width + up_width)]
    norm_size, bias_size = 4 * D // (2 * chips * groups), (4 * D + FF) // (2 * chips * groups)

    dp, z = lax.axis_index("dp"), lax.axis_index("seq")
    chip, core = dp // 2, dp % 2
    partner = {"dp": chip * 2 + (1 - core)}
    across = [{"dp": (chip + k) % chips * 2 + core} for k in range(chips)]
    along = [{"seq": (z + k) % groups} for k in range(groups)]

    def block(at, size):
        return pl.ds(pl.multiple_of(at * size, size), size)

    def remote(source, target, send, recv, at, peer):
        return pltpu.make_async_remote_copy(
            src_ref=source, dst_ref=target, send_sem=send.at[at], recv_sem=recv.at[at],
            device_id=peer, device_id_type=MESH,
        )

    started = []

    def send(*args):
        copy = remote(*args)
        copy.start()
        started.append(copy)
        return copy

    own_rows, own_toks = block(dp, depth), block(z, length)
    barrier = pltpu.get_barrier_semaphore()
    peers = [partner] + across[1:] + along[1:]
    for peer in peers:
        pl.semaphore_signal(barrier, inc=1, device_id=peer, device_id_type=MESH)
    w_all[own_rows, :in_width] = win_ref[...]
    w_all[own_rows, at_up:at_out] = wup_ref[...]
    w_all[own_rows, at_out:at_down] = wout_ref[...].astype(f32).T.astype(bf16)
    w_all[own_rows, at_down:] = wdown_ref[...].astype(f32).T.astype(bf16)
    x_all[own_toks, :] = x_ref[...]
    c_all[own_toks, :] = c_ref[...]
    s_mine[...] = jnp.zeros_like(s_mine)
    s_mine[: nrm_ref.shape[0], :] = nrm_ref[...].astype(f32)
    s_mine[nrm_ref.shape[0] : nrm_ref.shape[0] + bias_ref.shape[0], :] = bias_ref[...].astype(f32)
    s_all[dp, z] = s_mine[...]
    pl.semaphore_wait(barrier, len(peers))

    smalls = [send(s_mine, s_all.at[dp, z], z_send, z_recv, (0, k), along[k]) for k in range(1, groups)]
    weights, handed = {}, {}

    def send_piece(at):
        cols = pl.ds(*pieces[at])
        for k in range(1, chips):
            weights[at, k] = send(
                w_all.at[own_rows, cols], w_all.at[own_rows, cols], w_send, w_recv, (at, k), across[k]
            )
        handed[at] = [
            send(w_all.at[own_rows, cols], w_all.at[own_rows, cols], h_send, h_recv, (at, 0), partner)
        ]

    def take_piece(at):
        cols = pl.ds(*pieces[at])
        for k in range(1, chips):
            weights[at, k].wait_recv()
            came = block((chip + chips - k) % chips * 2 + core, depth)
            handed[at].append(
                send(w_all.at[came, cols], w_all.at[came, cols], h_send, h_recv, (at, k), partner)
            )
        for copy in handed[at]:
            copy.wait_recv()

    ways = [(-1, (z + 1) % groups, z < groups - 1), (1, (z + groups - 1) % groups, z > 0)]

    def row_copy(way, j):
        sign, to, _ = ways[way]
        at = block((z + groups + sign * j) % groups, length)
        return remote(x_all.at[at], x_all.at[at], x_send, x_recv, (way, j), {"seq": to})

    def holds(way, j):
        return z >= j if way == 0 else z + j < groups

    def pass_rows(j):
        for way in range(2):
            if j > 0:
                @pl.when(holds(way, j))
                def _():
                    row_copy(way, j - 1).wait_recv()
            if j < groups - 1:
                @pl.when(holds(way, j) & ways[way][2])
                def _():
                    row_copy(way, j).start()

    send_piece(0)
    pass_rows(0)
    for copy in smalls:
        copy.wait_recv()
    out = [send(s_all.at[dp], s_all.at[dp], s_send, s_recv, (0, k), across[k]) for k in range(1, chips)]
    over = [send(s_all.at[dp], s_all.at[dp], s_send, s_recv, (1, 0), partner)]
    for k in range(1, chips):
        out[k - 1].wait_recv()
        came = (chip + chips - k) % chips * 2 + core
        over.append(send(s_all.at[came], s_all.at[came], s_send, s_recv, (1, k), partner))
    for copy in over:
        copy.wait_recv()

    def owners(size, base, step, row, first):
        per, share = max(size // LANES, 1), max(LANES // size, 1)
        at = base // per * share + z * (step // per * share) + row // per * share
        return [((at + j) // groups, (at + j) % groups, first + row % per) for j in range(share)]

    def small_vector(size, base, step, count, first):
        parts = []
        for row in range(count):
            total = None
            for d_at, z_at, line in owners(size, base, step, row, first):
                value = s_all[d_at, z_at][line : line + 1, :]
                total = value if total is None else total + value
            parts.append(total)
        return jnp.concatenate(parts, axis=1)

    norm_vec = [small_vector(norm_size, r * (D // LANES), 0, D // LANES, 0) for r in range(4)]

    def normalise(values):
        centered = values - jnp.mean(values, axis=-1, keepdims=True)
        inv_std = lax.rsqrt(jnp.mean(centered * centered, axis=-1, keepdims=True) + norm_eps)
        return centered * inv_std, inv_std

    def norm_step(i):
        at = block(i, length)
        part, _ = normalise(x_all[at, :].astype(f32))
        normed[at, :] = part
        a_part = part * norm_vec[0] + norm_vec[1]
        m_part = part * norm_vec[2] + norm_vec[3]
        rows_a[at, :] = a_part.astype(bf16)
        rows_m[at, :] = m_part.astype(bf16)
        turned_a[:, at] = a_part.T.astype(bf16)
        turned_m[:, at] = m_part.T.astype(bf16)

    norm_step(z)
    for j in range(1, groups):
        pass_rows(j)
        if j == 2:
            take_piece(0)
            send_piece(1)
        if j == groups - 1:
            send_piece(2)
            c_moves = [
                send(c_ref, c_all.at[own_toks], z_send, z_recv, (2, k), along[k]) for k in range(1, groups)
            ]
        for way in range(2):
            @pl.when(holds(way, j))
            def _():
                norm_step((z + groups + ways[way][0] * j) % groups)

    in_bias = small_vector(bias_size, 0, in_width // LANES, in_width // LANES, 1)
    pair = 6 * HD

    def turn(values, sign):
        return (
            values * keep_ref[...]
            + sign * (pltpu.roll(values, pair - ROT // 2, 1) * right_ref[...])
            + sign * (pltpu.roll(values, ROT // 2, 1) * left_ref[...])
        )

    for two in range(heads // 2):
        cols = slice(two * pair, (two + 1) * pair)
        triple = mul(rows_a[...], w_all[:, cols], 1, 0) + in_bias[:, cols]
        triple = turn(triple, 1.0)
        for j in range(2):
            h = two * 2 + j
            q_s[h] = triple[:, j * 192 : j * 192 + 64].astype(bf16)
            k_s[h] = triple[:, j * 192 + 64 : j * 192 + 128].astype(bf16)
            v_s[h] = triple[:, j * 192 + 128 : j * 192 + 192].astype(bf16)

    step_rows = 128
    scale = HD ** (-0.5)

    def attend(h):
        for b in range(tok_len // step_rows):
            at, seen = slice(b * step_rows, (b + 1) * step_rows), (b + 1) * step_rows
            scores = mul(q_s[h, at, :], k_s[h, :seen, :], 1, 1) * scale
            q_pos = lax.broadcasted_iota(jnp.int32, scores.shape, 0) + b * step_rows
            k_pos = lax.broadcasted_iota(jnp.int32, scores.shape, 1)
            scores = jnp.where(q_pos >= k_pos, scores, masked_score)
            row_max = jnp.max(scores, axis=-1, keepdims=True)
            powers = jnp.exp(scores - row_max)
            part = powers * (1.0 / jnp.sum(powers, axis=-1, keepdims=True))
            probs[h, at, :seen] = part
            mixed_s[h, at, :] = mul(part.astype(bf16), v_s[h, :seen, :], 1, 0).astype(bf16)

    for h in range(heads):
        attend(h)
    both_rows[:, :out_width] = jnp.concatenate([mixed_s[h].astype(f32) for h in range(heads)], axis=1).astype(bf16)

    up_bias = small_vector(bias_size, 3 * D // LANES, up_width // LANES, up_width // LANES, 1)
    take_piece(1)
    wide = 256
    for j in range(up_width // wide):
        cols = slice(j * wide, (j + 1) * wide)
        up_cols = slice(at_up + j * wide, at_up + (j + 1) * wide)
        hidden = mul(rows_m[...], w_all[:, up_cols], 1, 0) + up_bias[:, cols]
        half = 0.5 * (1.0 + lax.erf(hidden * (1.0 / math.sqrt(2.0))))
        both_rows[:, out_width + j * wide : out_width + (j + 1) * wide] = (hidden * half).astype(bf16)
        slope[:, cols] = half + hidden * jnp.exp(-0.5 * hidden * hidden) * (1.0 / math.sqrt(2.0 * math.pi))

    take_piece(2)
    p_moves = []
    for k in list(range(1, groups)) + [0]:
        at = block((z + k) % groups, length)
        part = mul(both_rows[at, :], w_all[:, at_out:], 1, 1)
        p_out[k] = part.astype(bf16)
        if k > 0:
            p_moves.append(send(p_out.at[k], p_got.at[k - 1], z_send, z_recv, (3, k), along[k]))

    for copy in c_moves:
        copy.wait_recv()

    def turn_cot(i, carry):
        at = block(i, length)
        turned_c[:, at] = c_all[at, :].astype(f32).T.astype(bf16)
        return carry

    lax.fori_loop(0, groups, turn_cot, 0)
    halves, sums = {}, {}
    order = list(range(1, chips)) + [0]

    def give(at):
        cols = pl.ds(*pieces[at])
        for k in order:
            rows = block((chip + k) % chips * 2 + 1 - core, depth)
            halves[at, k] = send(
                g.at[rows, cols], g_half.at[k, :, cols], gh_send, gh_recv, (at, k), partner
            )

    def add(at):
        cols = pl.ds(*pieces[at])
        for k in order:
            rows = block((chip + k) % chips * 2 + core, depth)
            halves[at, k].wait_recv()
            both = g[rows, cols].astype(f32) + g_half[k, :, cols].astype(f32)
            if k > 0:
                g_sum[k - 1, :, cols] = both.astype(bf16)
                sums[at, k] = send(
                    g_sum.at[k - 1, :, cols], g_got.at[k - 1, :, cols], ga_send, ga_recv, (at, k), across[k]
                )
            else:
                g_out[:, cols] = both

    def finish(at):
        cols = pl.ds(*pieces[at])
        total = g_out[:, cols]
        for k in range(1, chips):
            sums[at, k].wait_recv()
            total = total + g_got[k - 1, :, cols].astype(f32)
        if at == 0:
            gi_ref[...] = total
        elif at == 1:
            gu_ref[...] = total
        else:
            go_ref[...] = total[:, :out_width].T
            gd_ref[...] = total[:, out_width:].T

    for j in range((out_width + up_width) // wide):
        cols = slice(j * wide, (j + 1) * wide)
        g[:, at_out + j * wide : at_out + (j + 1) * wide] = mul(turned_c[...], both_rows[:, cols], 1, 0).astype(bf16)
    give(2)

    up_sums = []
    for j in range(up_width // wide):
        cols = slice(j * wide, (j + 1) * wide)
        part = mul(c_all[...], w_all[:, at_down + j * wide : at_down + (j + 1) * wide], 1, 0) * slope[:, cols]
        part = part.astype(bf16)
        hid_grad[:, cols] = part
        up_sums.append(jnp.sum(part.astype(f32), axis=0, keepdims=True))
    add(2)
    for j in range(up_width // wide):
        cols = slice(j * wide, (j + 1) * wide)
        g[:, at_up + j * wide : at_up + (j + 1) * wide] = mul(turned_m[...], hid_grad[:, cols], 1, 0).astype(bf16)
    give(1)

    mixed_grad = mul(c_all[...], w_all[:, at_out:at_down], 1, 0).astype(bf16)
    for h in range(heads):
        mg_s[h] = mixed_grad[:, h * HD : (h + 1) * HD]
    add(1)

    def attend_back(h):
        for b in range(tok_len // step_rows):
            at, seen = slice(b * step_rows, (b + 1) * step_rows), (b + 1) * step_rows
            part, m_grad = probs[h, at, :seen], mg_s[h, at, :]
            p_grad = mul(m_grad, v_s[h, :seen, :], 1, 1)
            row_dot = jnp.sum(part * p_grad, axis=-1, keepdims=True)
            s_grad = (part * (p_grad - row_dot)).astype(bf16)
            dq_s[h % 2, at, :] = mul(s_grad, k_s[h, :seen, :], 1, 0) * scale
            low_p[at, :seen] = part.astype(bf16)
            low_ds[at, :seen] = s_grad
        for b in range(tok_len // step_rows):
            at, late = slice(b * step_rows, (b + 1) * step_rows), slice(b * step_rows, tok_len)
            dk_s[h % 2, at, :] = mul(low_ds[late, at], q_s[h, late, :], 0, 0) * scale
            dv_s[h % 2, at, :] = mul(low_p[late, at], mg_s[h, late, :], 0, 0)

    in_sums = []
    for two in range(heads // 2):
        joined = []
        for j in range(2):
            attend_back(two * 2 + j)
            joined += [dq_s[j], dk_s[j], dv_s[j]]
        part = turn(jnp.concatenate(joined, axis=1), -1.0).astype(bf16)
        tg[:, two * pair : (two + 1) * pair] = part
        in_sums.append(jnp.sum(part.astype(f32), axis=0, keepdims=True))

    norm_sums = None
    n_moves = []
    for k in list(range(1, groups)) + [0]:
        at = block((z + k) % groups, length)
        a_grad = mul(tg[at, :], w_all[:, :in_width], 1, 1)
        m_grad = mul(hid_grad[at, :], w_all[:, at_up:at_out], 1, 1)
        n_out[k] = (a_grad * norm_vec[0] + m_grad * norm_vec[2]).astype(bf16)
        if k > 0:
            n_moves.append(send(n_out.at[k], n_got.at[k - 1], z_send, z_recv, (4, k), along[k]))
        part = normed[at, :]
        terms = [a_grad * part, a_grad, m_grad * part, m_grad]
        terms = [jnp.sum(term, axis=0, keepdims=True) for term in terms]
        norm_sums = terms if norm_sums is None else [a + b for a, b in zip(norm_sums, terms)]

    for j in range(in_width // wide):
        cols = slice(j * wide, (j + 1) * wide)
        g[:, cols] = mul(turned_a[...], tg[:, cols], 1, 0).astype(bf16)
    give(0)

    v_mine[...] = jnp.zeros_like(v_mine)

    def place(vector, size, base, step, first):
        for row in range(vector.shape[1] // LANES):
            for d_at, z_at, line in owners(size, base, step, row, first):
                v_mine[d_at, z_at, line : line + 1, :] = vector[:, row * LANES : (row + 1) * LANES]

    for r in range(4):
        place(norm_sums[r], norm_size, r * (D // LANES), 0, 0)
    place(jnp.concatenate(in_sums, axis=1), bias_size, 0, in_width // LANES, 1)
    place(jnp.concatenate(up_sums, axis=1), bias_size, 3 * D // LANES, up_width // LANES, 1)
    cot_own = c_ref[...].astype(f32)
    place(jnp.sum(cot_own, axis=0, keepdims=True), bias_size, (3 * D + FF) // LANES, 0, 1)
    v_give = [
        send(v_mine.at[(chip + k) % chips * 2 + 1 - core], v_half.at[k], v_send, v_recv, (0, k), partner)
        for k in range(chips)
    ]
    add(0)
    finish(2)
    v_across = []
    for k in order:
        v_give[k].wait_recv()
        v_sum[k] = v_mine[(chip + k) % chips * 2 + core] + v_half[k]
        if k > 0:
            v_across.append(send(v_sum.at[k], v_got.at[k], v_send, v_recv, (1, k), across[k]))

    for copy in p_moves:
        copy.wait_recv()
    out_bias = small_vector(bias_size, (3 * D + FF) // LANES, 0, D // LANES, 1)
    own = x_ref[...].astype(f32)
    total = p_out[0].astype(f32)
    for k in range(1, groups):
        total = total + p_got[k - 1].astype(f32)
    lay_ref[...] = (own + total + out_bias).astype(bf16)

    total = v_sum[0]
    for copy in v_across:
        copy.wait_recv()
    for k in range(1, chips):
        total = total + v_got[k]
    v_all[...] = total
    v_along = [
        send(v_all.at[(z + k) % groups], v_last.at[k], z_send, z_recv, (5, k), along[k])
        for k in range(1, groups)
    ]

    finish(1)

    for copy in n_moves:
        copy.wait_recv()
    own_normed, own_std = normalise(own)
    total = n_out[0].astype(f32)
    for k in range(1, groups):
        total = total + n_got[k - 1].astype(f32)
    term = own_std * (
        total
        - jnp.mean(total, axis=-1, keepdims=True)
        - own_normed * jnp.mean(total * own_normed, axis=-1, keepdims=True)
    )
    gin_ref[...] = (cot_own + term).astype(bf16)

    for copy in v_along:
        copy.wait_recv()
    total = v_all[z]
    for k in range(1, groups):
        total = total + v_last[k]
    v_out[...] = total

    finish(0)
    for way in range(2):
        for j in range(groups - 1):
            @pl.when(holds(way, j) & ways[way][2])
            def _():
                row_copy(way, j).wait_send()
    for copy in started:
        copy.wait_send()


def layer(weights, x, c, smalls, tables, chips, groups):
    vm = pl.BlockSpec(memory_space=pltpu.VMEM)
    dma = pltpu.SemaphoreType.DMA
    length, depth, width = x.shape[0], weights[0].shape[0], (4 * D + 2 * FF) // groups
    tok_len, devices, heads = length * groups, 2 * chips, H // groups
    up_width, in_width = FF // groups, 3 * D // groups
    shape, rows, head = (tok_len, D), (groups, length, D), (heads, tok_len, HD)
    late, two_heads, tile = (groups - 1, length, D), (2, tok_len, HD), (8, LANES)
    buffers = [
        ((D, width), bf16), (shape, bf16), (shape, bf16), ((devices, groups) + tile, f32),
        (shape, f32), (shape, bf16), (shape, bf16),
        ((D, tok_len), bf16), ((D, tok_len), bf16), ((D, tok_len), bf16),
        (head, bf16), (head, bf16), (head, bf16), ((heads, tok_len, tok_len), f32), (head, bf16),
        ((tok_len, heads * HD + up_width), bf16), ((tok_len, up_width), f32),
        ((tok_len, up_width), bf16), (head, bf16), (two_heads, f32), (two_heads, f32), (two_heads, f32),
        ((tok_len, tok_len), bf16), ((tok_len, tok_len), bf16),
        ((tok_len, in_width), bf16),
        (rows, bf16), (late, bf16), (rows, bf16), (late, bf16),
        ((D, width), bf16), ((chips, depth, width), bf16), ((chips - 1, depth, width), bf16),
        ((chips - 1, depth, width), bf16),
        ((devices, groups) + tile, f32), ((chips, groups) + tile, f32), ((chips, groups) + tile, f32),
        ((chips, groups) + tile, f32), ((groups,) + tile, f32), ((groups,) + tile, f32),
        ((depth, width), f32), (tile, f32),
    ]
    sems = [(3, chips)] * 4 + [(2, chips)] * 2 + [(6, groups)] * 2 + [(2, groups)] * 2 + [(3, chips)] * 4 + [(2, chips)] * 2
    return pl.pallas_call(
        functools.partial(layer_kernel, chips, groups),
        out_shape=(
            jax.ShapeDtypeStruct(x.shape, bf16),
            jax.ShapeDtypeStruct(x.shape, bf16),
            *[jax.ShapeDtypeStruct(weight.shape, f32) for weight in weights],
            jax.ShapeDtypeStruct(tile, f32),
        ),
        in_specs=[vm] * 11,
        out_specs=(vm,) * 7,
        scratch_shapes=[pltpu.VMEM(*buffer) for buffer in buffers] + [dma(sem) for sem in sems],
        compiler_params=pltpu.CompilerParams(
            collective_id=0, has_side_effects=True, vmem_limit_bytes=60 * 2**20
        ),
        name="layer",
    )(*weights, x, c, *smalls, *tables)


def body(hidden_in, out_grad, norm_params, biases, attn_in, attn_out, mlp_up, mlp_down):
    groups, devices = lax.axis_size("seq"), lax.axis_size("dp")
    chips = devices // 2
    length = hidden_in.shape[1]
    norm_size, bias_size = norm_params.shape[0], biases.shape[0]
    flat = lax.axis_index("dp") * groups + lax.axis_index("seq")

    def tile_rows(values):
        size = values.shape[0]
        if size >= LANES:
            return values.reshape(size // LANES, LANES)
        offset = flat % (LANES // size) * size
        return lax.dynamic_update_slice(jnp.zeros((LANES,), values.dtype), values, (offset,))[None]

    def from_rows(rows, size):
        if size >= LANES:
            return rows.reshape(size)
        return lax.dynamic_slice(rows.reshape(LANES), (flat % (LANES // size) * size,), (size,))

    smalls = (tile_rows(norm_params), tile_rows(biases))
    norm_lines, bias_lines = smalls[0].shape[0], smalls[1].shape[0]
    layer_out, grad_input, grad_in, grad_out, grad_up, grad_down, sums = layer(
        (attn_in, attn_out, mlp_up, mlp_down),
        hidden_in[0],
        out_grad[0],
        smalls,
        rotary_tables(length * groups),
        chips,
        groups,
    )
    return (
        layer_out[None],
        grad_input[None],
        from_rows(sums[:norm_lines], norm_size),
        from_rows(sums[norm_lines : norm_lines + bias_lines], bias_size),
        grad_in,
        grad_out,
        grad_up,
        grad_down,
    )


def solution(mesh):
    in_specs = (
        P("dp", "seq", None),
        P("dp", "seq", None),
        P(("dp", "seq")),
        P(("dp", "seq")),
        P("dp", "seq"),
        P("seq", "dp"),
        P("dp", "seq"),
        P("seq", "dp"),
    )
    out_specs = (
        P("dp", "seq", None),
        P("dp", "seq", None),
        P(("dp", "seq")),
        P(("dp", "seq")),
        P("dp", "seq"),
        P("seq", "dp"),
        P("dp", "seq"),
        P("seq", "dp"),
    )
    return jax.shard_map(body, mesh=mesh, in_specs=in_specs, out_specs=out_specs, check_vma=False)
```

```python
import functools
import math

import jax
import jax.numpy as jnp
import numpy as np
from jax import lax
from jax.experimental import pallas as pl
from jax.experimental.pallas import tpu as pltpu
from jax.sharding import PartitionSpec as P

D = 1024
H = 16
HD = 64
FF = 4096
ROT = 16
LANES = 128

norm_eps = 1e-05
masked_score = -1e30
MESH = pl.DeviceIdType.MESH
f32, bf16 = jnp.float32, jnp.bfloat16


def rotary_tables(tok_len):
    half = ROT // 2
    frequency = np.power(np.float32(10000.0), np.float32(-2.0) * np.arange(half, dtype=np.float32) / np.float32(ROT))
    angles = np.arange(tok_len, dtype=np.float32)[:, None] * frequency.astype(np.float32)[None, :]
    cosine, sine = np.cos(angles.astype(np.float64)), np.sin(angles.astype(np.float64))
    keep = np.ones((tok_len, 2, 3, HD), np.float32)
    right = np.zeros((tok_len, 2, 3, HD), np.float32)
    left = np.zeros((tok_len, 2, 3, HD), np.float32)
    for part in range(2):
        keep[:, :, part, :half] = cosine[:, None]
        keep[:, :, part, half:ROT] = cosine[:, None]
        right[:, :, part, :half] = -sine[:, None]
        left[:, :, part, half:ROT] = sine[:, None]
    return [jnp.asarray(table.reshape(tok_len, 6 * HD)) for table in (keep, right, left)]


def mul(a, b, ca, cb):
    return lax.dot_general(a, b, (((ca,), (cb,)), ((), ())), preferred_element_type=f32)


def layer_kernel(
    chips, groups,
    win_ref, wout_ref, wup_ref, wdown_ref, x_ref, c_ref, nrm_ref, bias_ref, keep_ref, right_ref, left_ref,
    lay_ref, gin_ref, gi_ref, go_ref, gu_ref, gd_ref, vn_out, vb_out,
    w_all, x_all, c_all, s_all, normed, rows_a, rows_m, turned_a, turned_m, turned_c,
    q_s, k_s, v_s, probs, mixed_s, both_rows, slope, hid_grad, mg_s, dq_s, dk_s, dv_s, low_p, low_ds, tg,
    p_out, p_got, n_out, n_got, g, g_half, g_sum, g_got, v_mine, v_half, v_sum, v_got, v_all, v_last,
    g_out, s_mine, w_send, w_recv, h_send, h_recv, s_send, s_recv, z_send, z_recv, x_send, x_recv,
    gh_send, gh_recv, ga_send, ga_recv, v_send, v_recv,
):
    length, tok_len = x_ref.shape[0], x_all.shape[0]
    depth = win_ref.shape[0]
    heads = H // groups
    in_width, out_width, up_width = 3 * D // groups, D // groups, FF // groups
    at_up, at_out = in_width, in_width + up_width
    at_down, width = at_out + out_width, at_out + out_width + up_width
    pieces = [(0, in_width), (at_up, up_width), (at_out, out_width + up_width)]
    norm_size, bias_size = 4 * D // (2 * chips * groups), (4 * D + FF) // (2 * chips * groups)

    dp, z = lax.axis_index("dp"), lax.axis_index("seq")
    chip, core = dp // 2, dp % 2
    partner = {"dp": chip * 2 + (1 - core)}
    across = [{"dp": (chip + k) % chips * 2 + core} for k in range(chips)]
    along = [{"seq": (z + k) % groups} for k in range(groups)]

    def block(at, size):
        return pl.ds(pl.multiple_of(at * size, size), size)

    def remote(source, target, send, recv, at, peer):
        return pltpu.make_async_remote_copy(
            src_ref=source, dst_ref=target, send_sem=send.at[at], recv_sem=recv.at[at],
            device_id=peer, device_id_type=MESH,
        )

    started = []

    def send(*args):
        copy = remote(*args)
        copy.start()
        started.append(copy)
        return copy

    own_rows, own_toks = block(dp, depth), block(z, length)
    barrier = pltpu.get_barrier_semaphore()
    peers = [partner] + across[1:] + along[1:]
    for peer in peers:
        pl.semaphore_signal(barrier, inc=1, device_id=peer, device_id_type=MESH)
    w_all[own_rows, :in_width] = win_ref[...]
    w_all[own_rows, at_up:at_out] = wup_ref[...]
    w_all[own_rows, at_out:at_down] = wout_ref[...].astype(f32).T.astype(bf16)
    w_all[own_rows, at_down:] = wdown_ref[...].astype(f32).T.astype(bf16)
    x_all[own_toks, :] = x_ref[...]
    c_all[own_toks, :] = c_ref[...]
    s_mine[...] = jnp.zeros_like(s_mine)
    s_mine[: nrm_ref.shape[0], :] = nrm_ref[...].astype(f32)
    s_mine[nrm_ref.shape[0] : nrm_ref.shape[0] + bias_ref.shape[0], :] = bias_ref[...].astype(f32)
    s_all[dp, z] = s_mine[...]
    pl.semaphore_wait(barrier, len(peers))

    smalls = [send(s_mine, s_all.at[dp, z], z_send, z_recv, (0, k), along[k]) for k in range(1, groups)]
    weights, handed = {}, {}

    def send_piece(at):
        cols = pl.ds(*pieces[at])
        for k in range(1, chips):
            weights[at, k] = send(
                w_all.at[own_rows, cols], w_all.at[own_rows, cols], w_send, w_recv, (at, k), across[k]
            )
        handed[at] = [
            send(w_all.at[own_rows, cols], w_all.at[own_rows, cols], h_send, h_recv, (at, 0), partner)
        ]

    def take_piece(at):
        cols = pl.ds(*pieces[at])
        for k in range(1, chips):
            weights[at, k].wait_recv()
            came = block((chip + chips - k) % chips * 2 + core, depth)
            handed[at].append(
                send(w_all.at[came, cols], w_all.at[came, cols], h_send, h_recv, (at, k), partner)
            )
        for copy in handed[at]:
            copy.wait_recv()

    ways = [(-1, (z + 1) % groups, z < groups - 1), (1, (z + groups - 1) % groups, z > 0)]

    def row_copy(way, j):
        sign, to, _ = ways[way]
        at = block((z + groups + sign * j) % groups, length)
        return remote(x_all.at[at], x_all.at[at], x_send, x_recv, (way, j), {"seq": to})

    def holds(way, j):
        return z >= j if way == 0 else z + j < groups

    def pass_rows(j):
        for way in range(2):
            if j > 0:
                @pl.when(holds(way, j))
                def _():
                    row_copy(way, j - 1).wait_recv()
            if j < groups - 1:
                @pl.when(holds(way, j) & ways[way][2])
                def _():
                    row_copy(way, j).start()

    send_piece(0)
    pass_rows(0)
    for copy in smalls:
        copy.wait_recv()
    out = [send(s_all.at[dp], s_all.at[dp], s_send, s_recv, (0, k), across[k]) for k in range(1, chips)]
    over = [send(s_all.at[dp], s_all.at[dp], s_send, s_recv, (1, 0), partner)]
    for k in range(1, chips):
        out[k - 1].wait_recv()
        came = (chip + chips - k) % chips * 2 + core
        over.append(send(s_all.at[came], s_all.at[came], s_send, s_recv, (1, k), partner))
    for copy in over:
        copy.wait_recv()

    def owners(size, base, step, row, first):
        per, share = max(size // LANES, 1), max(LANES // size, 1)
        at = base // per * share + z * (step // per * share) + row // per * share
        return [((at + j) // groups, (at + j) % groups, first + row % per) for j in range(share)]

    def small_vector(size, base, step, count, first):
        parts = []
        for row in range(count):
            total = None
            for d_at, z_at, line in owners(size, base, step, row, first):
                value = s_all[d_at, z_at][line : line + 1, :]
                total = value if total is None else total + value
            parts.append(total)
        return jnp.concatenate(parts, axis=1)

    norm_vec = [small_vector(norm_size, r * (D // LANES), 0, D // LANES, 0) for r in range(4)]

    def normalise(values):
        centered = values - jnp.mean(values, axis=-1, keepdims=True)
        inv_std = lax.rsqrt(jnp.mean(centered * centered, axis=-1, keepdims=True) + norm_eps)
        return centered * inv_std, inv_std

    def norm_step(i):
        at = block(i, length)
        part, _ = normalise(x_all[at, :].astype(f32))
        normed[at, :] = part
        a_part = part * norm_vec[0] + norm_vec[1]
        m_part = part * norm_vec[2] + norm_vec[3]
        rows_a[at, :] = a_part.astype(bf16)
        rows_m[at, :] = m_part.astype(bf16)
        turned_a[:, at] = a_part.T.astype(bf16)
        turned_m[:, at] = m_part.T.astype(bf16)

    norm_step(z)
    for j in range(1, groups):
        pass_rows(j)
        if j == 2:
            take_piece(0)
            send_piece(1)
        if j == groups - 1:
            send_piece(2)
            c_moves = [
                send(c_ref, c_all.at[own_toks], z_send, z_recv, (2, k), along[k]) for k in range(1, groups)
            ]
        for way in range(2):
            @pl.when(holds(way, j))
            def _():
                norm_step((z + groups + ways[way][0] * j) % groups)

    in_bias = small_vector(bias_size, 0, in_width // LANES, in_width // LANES, 1)
    pair = 6 * HD

    def turn(values, sign):
        return (
            values * keep_ref[...]
            + sign * (pltpu.roll(values, pair - ROT // 2, 1) * right_ref[...])
            + sign * (pltpu.roll(values, ROT // 2, 1) * left_ref[...])
        )

    for two in range(heads // 2):
        cols = slice(two * pair, (two + 1) * pair)
        triple = mul(rows_a[...], w_all[:, cols], 1, 0) + in_bias[:, cols]
        triple = turn(triple, 1.0)
        for j in range(2):
            h = two * 2 + j
            q_s[h] = triple[:, j * 192 : j * 192 + 64].astype(bf16)
            k_s[h] = triple[:, j * 192 + 64 : j * 192 + 128].astype(bf16)
            v_s[h] = triple[:, j * 192 + 128 : j * 192 + 192].astype(bf16)

    step_rows = 128
    scale = HD ** (-0.5)

    def attend(h):
        for b in range(tok_len // step_rows):
            at, seen = slice(b * step_rows, (b + 1) * step_rows), (b + 1) * step_rows
            scores = mul(q_s[h, at, :], k_s[h, :seen, :], 1, 1) * scale
            q_pos = lax.broadcasted_iota(jnp.int32, scores.shape, 0) + b * step_rows
            k_pos = lax.broadcasted_iota(jnp.int32, scores.shape, 1)
            scores = jnp.where(q_pos >= k_pos, scores, masked_score)
            row_max = jnp.max(scores, axis=-1, keepdims=True)
            powers = jnp.exp(scores - row_max)
            part = powers * (1.0 / jnp.sum(powers, axis=-1, keepdims=True))
            probs[h, at, :seen] = part
            mixed_s[h, at, :] = mul(part.astype(bf16), v_s[h, :seen, :], 1, 0).astype(bf16)

    for h in range(heads):
        attend(h)
    both_rows[:, :out_width] = jnp.concatenate([mixed_s[h].astype(f32) for h in range(heads)], axis=1).astype(bf16)

    up_bias = small_vector(bias_size, 3 * D // LANES, up_width // LANES, up_width // LANES, 1)
    take_piece(1)
    wide = 256
    for j in range(up_width // wide):
        cols = slice(j * wide, (j + 1) * wide)
        up_cols = slice(at_up + j * wide, at_up + (j + 1) * wide)
        hidden = mul(rows_m[...], w_all[:, up_cols], 1, 0) + up_bias[:, cols]
        half = 0.5 * (1.0 + lax.erf(hidden * (1.0 / math.sqrt(2.0))))
        both_rows[:, out_width + j * wide : out_width + (j + 1) * wide] = (hidden * half).astype(bf16)
        slope[:, cols] = half + hidden * jnp.exp(-0.5 * hidden * hidden) * (1.0 / math.sqrt(2.0 * math.pi))

    take_piece(2)
    p_moves = []
    for k in list(range(1, groups)) + [0]:
        at = block((z + k) % groups, length)
        part = mul(both_rows[at, :], w_all[:, at_out:], 1, 1)
        p_out[k] = part.astype(bf16)
        if k > 0:
            p_moves.append(send(p_out.at[k], p_got.at[k - 1], z_send, z_recv, (3, k), along[k]))

    for copy in c_moves:
        copy.wait_recv()

    def turn_cot(i, carry):
        at = block(i, length)
        turned_c[:, at] = c_all[at, :].astype(f32).T.astype(bf16)
        return carry

    lax.fori_loop(0, groups, turn_cot, 0)
    halves, sums = {}, {}
    order = list(range(1, chips)) + [0]

    def give(at):
        cols = pl.ds(*pieces[at])
        for k in order:
            rows = block((chip + k) % chips * 2 + 1 - core, depth)
            halves[at, k] = send(
                g.at[rows, cols], g_half.at[k, :, cols], gh_send, gh_recv, (at, k), partner
            )

    def add(at):
        cols = pl.ds(*pieces[at])
        for k in order:
            rows = block((chip + k) % chips * 2 + core, depth)
            halves[at, k].wait_recv()
            both = g[rows, cols].astype(f32) + g_half[k, :, cols].astype(f32)
            if k > 0:
                g_sum[k - 1, :, cols] = both.astype(bf16)
                sums[at, k] = send(
                    g_sum.at[k - 1, :, cols], g_got.at[k - 1, :, cols], ga_send, ga_recv, (at, k), across[k]
                )
            else:
                g_out[:, cols] = both

    def finish(at):
        cols = pl.ds(*pieces[at])
        total = g_out[:, cols]
        for k in range(1, chips):
            sums[at, k].wait_recv()
            total = total + g_got[k - 1, :, cols].astype(f32)
        if at == 0:
            gi_ref[...] = total
        elif at == 1:
            gu_ref[...] = total
        else:
            go_ref[...] = total[:, :out_width].T
            gd_ref[...] = total[:, out_width:].T

    for j in range((out_width + up_width) // wide):
        cols = slice(j * wide, (j + 1) * wide)
        g[:, at_out + j * wide : at_out + (j + 1) * wide] = mul(turned_c[...], both_rows[:, cols], 1, 0).astype(bf16)
    give(2)

    up_sums = []
    for j in range(up_width // wide):
        cols = slice(j * wide, (j + 1) * wide)
        part = mul(c_all[...], w_all[:, at_down + j * wide : at_down + (j + 1) * wide], 1, 0) * slope[:, cols]
        part = part.astype(bf16)
        hid_grad[:, cols] = part
        up_sums.append(jnp.sum(part.astype(f32), axis=0, keepdims=True))
    add(2)

    mixed_grad = mul(c_all[...], w_all[:, at_out:at_down], 1, 0).astype(bf16)
    for h in range(heads):
        mg_s[h] = mixed_grad[:, h * HD : (h + 1) * HD]

    def attend_back(h):
        for b in range(tok_len // step_rows):
            at, seen = slice(b * step_rows, (b + 1) * step_rows), (b + 1) * step_rows
            part, m_grad = probs[h, at, :seen], mg_s[h, at, :]
            p_grad = mul(m_grad, v_s[h, :seen, :], 1, 1)
            row_dot = jnp.sum(part * p_grad, axis=-1, keepdims=True)
            s_grad = (part * (p_grad - row_dot)).astype(bf16)
            dq_s[h % 2, at, :] = mul(s_grad, k_s[h, :seen, :], 1, 0) * scale
            low_p[at, :seen] = part.astype(bf16)
            low_ds[at, :seen] = s_grad
        for b in range(tok_len // step_rows):
            at, late = slice(b * step_rows, (b + 1) * step_rows), slice(b * step_rows, tok_len)
            dk_s[h % 2, at, :] = mul(low_ds[late, at], q_s[h, late, :], 0, 0) * scale
            dv_s[h % 2, at, :] = mul(low_p[late, at], mg_s[h, late, :], 0, 0)

    in_sums = []
    for two in range(heads // 2):
        joined = []
        for j in range(2):
            attend_back(two * 2 + j)
            joined += [dq_s[j], dk_s[j], dv_s[j]]
        part = turn(jnp.concatenate(joined, axis=1), -1.0).astype(bf16)
        tg[:, two * pair : (two + 1) * pair] = part
        in_sums.append(jnp.sum(part.astype(f32), axis=0, keepdims=True))

    norm_sums = None
    n_moves = []
    for k in list(range(1, groups)) + [0]:
        at = block((z + k) % groups, length)
        a_grad = mul(tg[at, :], w_all[:, :in_width], 1, 1)
        m_grad = mul(hid_grad[at, :], w_all[:, at_up:at_out], 1, 1)
        n_out[k] = (a_grad * norm_vec[0] + m_grad * norm_vec[2]).astype(bf16)
        if k > 0:
            n_moves.append(send(n_out.at[k], n_got.at[k - 1], z_send, z_recv, (4, k), along[k]))
        part = normed[at, :]
        terms = [a_grad * part, a_grad, m_grad * part, m_grad]
        terms = [jnp.sum(term, axis=0, keepdims=True) for term in terms]
        norm_sums = terms if norm_sums is None else [a + b for a, b in zip(norm_sums, terms)]

    for j in range(up_width // wide):
        cols = slice(j * wide, (j + 1) * wide)
        g[:, at_up + j * wide : at_up + (j + 1) * wide] = mul(turned_m[...], hid_grad[:, cols], 1, 0).astype(bf16)
    give(1)
    for j in range(in_width // wide):
        cols = slice(j * wide, (j + 1) * wide)
        g[:, cols] = mul(turned_a[...], tg[:, cols], 1, 0).astype(bf16)
    give(0)
    add(1)

    v_mine[...] = jnp.zeros_like(v_mine)

    def place(vector, size, base, step, first):
        for row in range(vector.shape[1] // LANES):
            for d_at, z_at, line in owners(size, base, step, row, first):
                v_mine[d_at, z_at, line : line + 1, :] = vector[:, row * LANES : (row + 1) * LANES]

    for r in range(4):
        place(norm_sums[r], norm_size, r * (D // LANES), 0, 0)
    place(jnp.concatenate(in_sums, axis=1), bias_size, 0, in_width // LANES, 1)
    place(jnp.concatenate(up_sums, axis=1), bias_size, 3 * D // LANES, up_width // LANES, 1)
    cot_own = c_ref[...].astype(f32)
    place(jnp.sum(cot_own, axis=0, keepdims=True), bias_size, (3 * D + FF) // LANES, 0, 1)
    v_give = [
        send(v_mine.at[(chip + k) % chips * 2 + 1 - core], v_half.at[k], v_send, v_recv, (0, k), partner)
        for k in range(chips)
    ]
    add(0)
    finish(2)
    v_across = []
    for k in order:
        v_give[k].wait_recv()
        v_sum[k] = v_mine[(chip + k) % chips * 2 + core] + v_half[k]
        if k > 0:
            v_across.append(send(v_sum.at[k], v_got.at[k], v_send, v_recv, (1, k), across[k]))

    for copy in p_moves:
        copy.wait_recv()
    out_bias = small_vector(bias_size, (3 * D + FF) // LANES, 0, D // LANES, 1)
    own = x_ref[...].astype(f32)
    total = p_out[0].astype(f32)
    for k in range(1, groups):
        total = total + p_got[k - 1].astype(f32)
    lay_ref[...] = (own + total + out_bias).astype(bf16)

    total = v_sum[0]
    for copy in v_across:
        copy.wait_recv()
    for k in range(1, chips):
        total = total + v_got[k]
    v_all[...] = total
    v_along = [
        send(v_all.at[(z + k) % groups], v_last.at[k], z_send, z_recv, (5, k), along[k])
        for k in range(1, groups)
    ]

    finish(1)

    for copy in n_moves:
        copy.wait_recv()
    own_normed, own_std = normalise(own)
    total = n_out[0].astype(f32)
    for k in range(1, groups):
        total = total + n_got[k - 1].astype(f32)
    term = own_std * (
        total
        - jnp.mean(total, axis=-1, keepdims=True)
        - own_normed * jnp.mean(total * own_normed, axis=-1, keepdims=True)
    )
    gin_ref[...] = (cot_own + term).astype(bf16)

    for copy in v_along:
        copy.wait_recv()
    total = v_all[z]
    for k in range(1, groups):
        total = total + v_last[k]
    norm_lines = nrm_ref.shape[0]
    vn_out[...] = total[:norm_lines]
    vb_out[...] = total[norm_lines : norm_lines + bias_ref.shape[0]]

    finish(0)
    for way in range(2):
        for j in range(groups - 1):
            @pl.when(holds(way, j) & ways[way][2])
            def _():
                row_copy(way, j).wait_send()
    for copy in started:
        copy.wait_send()


def layer(weights, x, c, smalls, tables, chips, groups):
    vm = pl.BlockSpec(memory_space=pltpu.VMEM)
    dma = pltpu.SemaphoreType.DMA
    length, depth, width = x.shape[0], weights[0].shape[0], (4 * D + 2 * FF) // groups
    tok_len, devices, heads = length * groups, 2 * chips, H // groups
    up_width, in_width = FF // groups, 3 * D // groups
    shape, rows, head = (tok_len, D), (groups, length, D), (heads, tok_len, HD)
    late, two_heads, tile = (groups - 1, length, D), (2, tok_len, HD), (8, LANES)
    buffers = [
        ((D, width), bf16), (shape, bf16), (shape, bf16), ((devices, groups) + tile, f32),
        (shape, f32), (shape, bf16), (shape, bf16),
        ((D, tok_len), bf16), ((D, tok_len), bf16), ((D, tok_len), bf16),
        (head, bf16), (head, bf16), (head, bf16), ((heads, tok_len, tok_len), f32), (head, bf16),
        ((tok_len, heads * HD + up_width), bf16), ((tok_len, up_width), f32),
        ((tok_len, up_width), bf16), (head, bf16), (two_heads, f32), (two_heads, f32), (two_heads, f32),
        ((tok_len, tok_len), bf16), ((tok_len, tok_len), bf16),
        ((tok_len, in_width), bf16),
        (rows, bf16), (late, bf16), (rows, bf16), (late, bf16),
        ((D, width), bf16), ((chips, depth, width), bf16), ((chips - 1, depth, width), bf16),
        ((chips - 1, depth, width), bf16),
        ((devices, groups) + tile, f32), ((chips, groups) + tile, f32), ((chips, groups) + tile, f32),
        ((chips, groups) + tile, f32), ((groups,) + tile, f32), ((groups,) + tile, f32),
        ((depth, width), f32), (tile, f32),
    ]
    sems = [(3, chips)] * 4 + [(2, chips)] * 2 + [(6, groups)] * 2 + [(2, groups)] * 2 + [(3, chips)] * 4 + [(2, chips)] * 2
    return pl.pallas_call(
        functools.partial(layer_kernel, chips, groups),
        out_shape=(
            jax.ShapeDtypeStruct(x.shape, bf16),
            jax.ShapeDtypeStruct(x.shape, bf16),
            *[jax.ShapeDtypeStruct(weight.shape, f32) for weight in weights],
            *[jax.ShapeDtypeStruct(small.shape, f32) for small in smalls],
        ),
        in_specs=[vm] * 11,
        out_specs=(vm,) * 8,
        scratch_shapes=[pltpu.VMEM(*buffer) for buffer in buffers] + [dma(sem) for sem in sems],
        compiler_params=pltpu.CompilerParams(
            collective_id=0, has_side_effects=True, vmem_limit_bytes=60 * 2**20
        ),
        name="layer",
    )(*weights, x, c, *smalls, *tables)


def body(hidden_in, out_grad, norm_params, biases, attn_in, attn_out, mlp_up, mlp_down):
    groups, devices = lax.axis_size("seq"), lax.axis_size("dp")
    chips = devices // 2
    length = hidden_in.shape[1]
    norm_size, bias_size = norm_params.shape[0], biases.shape[0]
    flat = lax.axis_index("dp") * groups + lax.axis_index("seq")

    def tile_rows(values):
        size = values.shape[0]
        if size >= LANES:
            return values.reshape(size // LANES, LANES)
        offset = flat % (LANES // size) * size
        return lax.dynamic_update_slice(jnp.zeros((LANES,), values.dtype), values, (offset,))[None]

    def from_rows(rows, size):
        if size >= LANES:
            return rows.reshape(size)
        return lax.dynamic_slice(rows.reshape(LANES), (flat % (LANES // size) * size,), (size,))

    smalls = (tile_rows(norm_params), tile_rows(biases))
    layer_out, grad_input, grad_in, grad_out, grad_up, grad_down, norm_sums, bias_sums = layer(
        (attn_in, attn_out, mlp_up, mlp_down),
        hidden_in[0],
        out_grad[0],
        smalls,
        rotary_tables(length * groups),
        chips,
        groups,
    )
    return (
        layer_out[None],
        grad_input[None],
        from_rows(norm_sums, norm_size),
        from_rows(bias_sums, bias_size),
        grad_in,
        grad_out,
        grad_up,
        grad_down,
    )


def solution(mesh):
    in_specs = (
        P("dp", "seq", None),
        P("dp", "seq", None),
        P(("dp", "seq")),
        P(("dp", "seq")),
        P("dp", "seq"),
        P("seq", "dp"),
        P("dp", "seq"),
        P("seq", "dp"),
    )
    out_specs = (
        P("dp", "seq", None),
        P("dp", "seq", None),
        P(("dp", "seq")),
        P(("dp", "seq")),
        P("dp", "seq"),
        P("seq", "dp"),
        P("dp", "seq"),
        P("seq", "dp"),
    )
    return jax.shard_map(body, mesh=mesh, in_specs=in_specs, out_specs=out_specs, check_vma=False)
```
